256 devices in a mesh: rep: 16 (over z_hi, x, core), tp: 16 (over y, z_lo).
Axes of the slice: x: 4, y: 4, z: 8 (z_hi: 2, z_lo: 4; z = z_hi * 4 + z_lo), core: 2. Of those that a mesh axis runs over, the one named last changes fastest.
Arguments:
- trainer_weight: bfloat16 [32, 512, 256], P('rep', 'tp'), may hold values from -0.25 to 0.25
- bucket_slot: int32 [32], replicated, may hold values from 0 to 31, each once
- bucket_version: int32 [32], replicated, may hold values from 0 to 2
- replica_version: int32 [16, 32], P('rep'), may hold values from 0 to 2
- old_weight: bfloat16 [16, 512, 8192], P('rep', None, 'tp'), may hold values from -1 to 1
- old_scale: float32 [16, 4, 64], P('rep', None, 'tp'), may hold values from 0.08 to 0.3
- q_nope: bfloat16 [2, 16, 256, 4096], P(None, 'rep', None, 'tp'), may hold values from -6 to 6
- q_rope: bfloat16 [2, 16, 256, 2048], P(None, 'rep', None, 'tp'), may hold values from -80 to 80
- cache_latent: bfloat16 [16, 256, 384, 512], P('rep', 'tp'), may hold values from -6 to 6
- cache_rope: bfloat16 [16, 256, 24576], P('rep', 'tp'), may hold values from -16 to 16
- new_token: bfloat16 [2, 16, 256, 576], P(None, 'rep', 'tp'), may hold values from -6 to 6
- lengths: int32 [16, 256], P('rep', 'tp'), may hold values from 2 to 384, as said below
- out_weight: bfloat16 [4096, 7168], P('tp'), may hold values from -0.09375 to 0.09375
Outputs:
- served_weight: bfloat16 [16, 512, 8192], P('rep', None, 'tp')
- served_scale: float32 [16, 4, 64], P('rep', None, 'tp')
- decoded: bfloat16 [2, 16, 256, 7168], P(None, 'rep', 'tp')
The draws below stay inside these ranges and needn't reach their ends.
Inputs may be any that keep to these rules, and one draw needn't show every extreme that they name: `bucket_slot`: each slot holds exactly one head's bucket; slot k lies on rep index k // (32 / 16). `lengths`: every replica has a row of length 384.
All inputs are finite; a program needn't handle non-finite values. Where the reference program divides by a largest or mean magnitude, that divisor is 1e-20 or more.
Results may differ from the reference program's by a relative error of at most 0.027.
Values may be sent and summed in bfloat16 or wider, within the bound.
A program may use at most 128 MiB of HBM per device.

```python
import math
import jax
import jax.numpy as jnp
from jax import lax

D = 7168
HEADS = 32
LAT = 512
NOPE = 128
ROPE = 64
VDIM = 128
BLOCK = 128
STEPS = 2
ROWS = 256
LEN = 384
REPLICAS = 16


def rope_base(key):
    return jax.random.normal(jax.random.fold_in(key, 11), (REPLICAS, ROWS, LEN, ROPE), jnp.float32)


def draw_cache_rope(key, part):
    base = rope_base(key)
    return base.reshape(REPLICAS, ROWS, LEN * ROPE).astype(jnp.bfloat16)


def draw_q_rope(key, part):
    key = jax.random.fold_in(key, 7)
    values = jax.random.normal(key, (STEPS, REPLICAS, ROWS, HEADS, ROPE), jnp.float32)
    return values.reshape(STEPS, REPLICAS, ROWS, HEADS * ROPE).astype(jnp.bfloat16)


def draw_lengths(key, part):
    key = jax.random.fold_in(key, 23)
    values = jax.random.randint(key, (REPLICAS, ROWS), 2, LEN + 1)
    longest = jax.random.randint(jax.random.fold_in(key, 1), (REPLICAS, 1), 0, ROWS)
    return jnp.where(jnp.arange(ROWS)[None, :] == longest, LEN, values).astype(jnp.int32)


def place_ends(entries, stream_key, smallest, largest):
    shape = entries.shape
    spot = [jax.random.randint(jax.random.fold_in(stream_key, axis), (), 0, shape[axis]) for axis in range(len(shape))]
    entries = entries.at[tuple(spot)].set(smallest)
    longest = shape.index(max(shape))
    spot[longest] = (spot[longest] + 1) % shape[longest]
    return entries.at[tuple(spot)].set(largest)


def steps_of(own_key, extent, cuts, smallest, top_value):
    gain = 1.0
    for position, parts in cuts:
        heights = jax.random.uniform(jax.random.fold_in(jax.random.fold_in(own_key, 6), position), (parts,), jnp.float32, smallest / len(cuts), top_value / len(cuts))
        gain = gain * jnp.repeat(jnp.exp(heights), extent[position] // parts).reshape((-1,) + (1,) * (len(extent) - 1 - position))
    return gain


def centred(rng, shape, scale, reach, pieces=(), kind=jnp.bfloat16):
    drawn = jax.random.normal(rng, shape, jnp.float32) * scale
    if len(pieces) > 0:
        drawn = steps_of(rng, shape, pieces, -0.22, 0.18) * drawn
    return jnp.clip(drawn, min=-reach, max=reach).astype(kind)


def setup_inputs(seed: int = 0) -> dict:
    splits = jax.random.split(jax.random.key(seed), 14)
    return {
        "trainer_weight": centred(splits[0], (HEADS, LAT, NOPE + VDIM), LAT ** -0.5, 0.25, ((0, 16), (1, 16))),
        "bucket_slot": jax.random.permutation(splits[1], HEADS).astype(jnp.int32),
        "bucket_version": place_ends(jax.random.randint(splits[2], (HEADS,), 0, 3), jax.random.fold_in(splits[2], 1), 0, 2).astype(jnp.int32),
        "replica_version": place_ends(jax.random.randint(splits[3], (REPLICAS, HEADS), 0, 3), jax.random.fold_in(splits[3], 1), 0, 2).astype(jnp.int32),
        "old_weight": jnp.clip(jax.random.uniform(splits[4], (REPLICAS, LAT, HEADS * (NOPE + VDIM)), jnp.float32, -1.0, 1.0) * steps_of(splits[4], (REPLICAS, LAT, HEADS * (NOPE + VDIM)), ((0, 16), (2, 16)), -0.4, 0.0), -1.0, 1.0).astype(jnp.bfloat16),
        "old_scale": jnp.clip(jnp.exp(math.log(0.3) - 1.3217559 * jax.random.uniform(splits[5], (REPLICAS, LAT // BLOCK, HEADS * 2), jnp.float32) ** steps_of(splits[5], (REPLICAS, LAT // BLOCK, HEADS * 2), ((0, 16), (2, 16)), -0.2, 0.2)), 0.08, 0.3),
        "q_nope": centred(splits[6], (STEPS, REPLICAS, ROWS, HEADS * NOPE), 1.0, 6.0, ((1, 16), (3, 16))),
        "q_rope": draw_q_rope(jax.random.fold_in(splits[13], 71), 0),
        "cache_latent": centred(splits[8], (REPLICAS, ROWS, LEN, LAT), 1.0, 6.0, ((0, 16), (1, 16))),
        "cache_rope": draw_cache_rope(jax.random.fold_in(splits[13], 71), 0),
        "new_token": centred(splits[10], (STEPS, REPLICAS, ROWS, LAT + ROPE), 1.0, 6.0, ((1, 16), (2, 16))),
        "lengths": draw_lengths(jax.random.fold_in(splits[13], 71), 0),
        "out_weight": centred(splits[12], (HEADS * VDIM, D), (HEADS * VDIM) ** -0.5, 0.09375, ((0, 16),)),
    }


EPSILON = 1e-6


def attend(row_lat, row_rope, keys_lat, keys_rope, fresh_tok, lengths, step_idx):
    fresh_lat = fresh_tok[:, :, :LAT].astype(jnp.float32)
    fresh_rope = fresh_tok[:, :, LAT:].astype(jnp.float32)
    query_lat = row_lat.astype(jnp.float32)
    query_rope = row_rope.astype(jnp.float32)
    latents = keys_lat.astype(jnp.float32)
    scaling = (NOPE + ROPE) ** -0.5
    cached = jnp.einsum('rhl,rjl->rhj', query_lat, latents) + jnp.einsum('rhe,rje->rhj', query_rope, keys_rope.astype(jnp.float32))
    newest = jnp.einsum('rhl,rtl->rht', query_lat, fresh_lat) + jnp.einsum('rhe,rte->rht', query_rope, fresh_rope)
    scores = jnp.concatenate([cached, newest], axis=2) * scaling
    positions = keys_lat.shape[1]
    usable_cache = jnp.arange(positions, dtype=jnp.int32)[None, :] < lengths[:, None]
    usable_new = jnp.broadcast_to((jnp.arange(STEPS, dtype=jnp.int32) <= step_idx)[None, :], (keys_lat.shape[0], STEPS))
    usable = jnp.concatenate([usable_cache, usable_new], axis=1)[:, None, :]
    scores = jnp.where(usable, scores, -jnp.inf)
    row_max = jnp.max(scores, axis=2, keepdims=True)
    expped = jnp.exp(scores - row_max)
    weights_bf = (expped / jnp.sum(expped, axis=2, keepdims=True)).astype(jnp.bfloat16).astype(jnp.float32)
    attended = jnp.einsum('rhj,rjl->rhl', weights_bf[:, :, :positions], latents) + jnp.einsum('rht,rtl->rhl', weights_bf[:, :, positions:], fresh_lat)
    return attended.astype(jnp.bfloat16)


def reference(trainer_weight, bucket_slot, bucket_version, replica_version, old_weight, old_scale, q_nope, q_rope, cache_latent, cache_rope, new_token, lengths, out_weight):
    lat_blocks = LAT // BLOCK
    width = NOPE + VDIM
    buckets = jnp.take(trainer_weight, bucket_slot, axis=0).astype(jnp.float32)
    blocked = buckets.reshape(HEADS, lat_blocks, BLOCK, 2, BLOCK)
    block_scale = jnp.max(jnp.abs(blocked), axis=(2, 4)) + EPSILON
    fresh_quant = (blocked / block_scale[:, :, None, :, None]).astype(jnp.bfloat16)
    fresh_layout = jnp.transpose(fresh_quant.reshape(HEADS, LAT, width), (1, 0, 2)).reshape(LAT, HEADS * width)
    scale_layout = jnp.transpose(block_scale, (1, 0, 2)).reshape(lat_blocks, HEADS * 2)
    stale = replica_version != bucket_version[None, :]
    stale_cols = jnp.repeat(stale, width, axis=1)[:, None, :]
    stale_blocks = jnp.repeat(stale, 2, axis=1)[:, None, :]
    served_weight = jnp.where(stale_cols, fresh_layout[None], old_weight)
    served_scale = jnp.where(stale_blocks, scale_layout[None], old_scale)

    def replica_decode(bundle):
        served, scales, query_nope_all, query_rope_all, keys_lat, keys_rope_flat, fresh_all, row_lengths = bundle
        dequant = (served.astype(jnp.float32).reshape(lat_blocks, BLOCK, HEADS, 2, BLOCK) * scales.reshape(lat_blocks, 1, HEADS, 2, 1)).astype(jnp.bfloat16)
        dequant = dequant.reshape(LAT, HEADS, 2, BLOCK).astype(jnp.float32)
        key_map = dequant[:, :, 0, :]
        value_map = dequant[:, :, 1, :]
        fresh_tok = jnp.transpose(fresh_all, (1, 0, 2))
        keys_rope = keys_rope_flat.reshape(ROWS, LEN, ROPE)
        results = []
        for step_idx in range(STEPS):
            query_nope = query_nope_all[step_idx].reshape(ROWS, HEADS, NOPE).astype(jnp.float32)
            query_lat = jnp.einsum('rhn,lhn->rhl', query_nope, key_map).astype(jnp.bfloat16)
            query_rope = query_rope_all[step_idx].reshape(ROWS, HEADS, ROPE)
            attended = attend(query_lat, query_rope, keys_lat, keys_rope, fresh_tok, row_lengths, step_idx)
            heads_out = jnp.einsum('rhl,lhv->rhv', attended.astype(jnp.float32), value_map).astype(jnp.bfloat16)
            heads_out = heads_out.reshape(ROWS, HEADS * VDIM)
            results.append(jnp.dot(heads_out, out_weight, preferred_element_type=jnp.float32).astype(jnp.bfloat16))
        return jnp.stack(results)

    decoded = lax.map(replica_decode, (served_weight, served_scale, jnp.moveaxis(q_nope, 1, 0), jnp.moveaxis(q_rope, 1, 0), cache_latent, cache_rope, jnp.moveaxis(new_token, 1, 0), lengths))
    return served_weight, served_scale, jnp.moveaxis(decoded, 0, 1)
```

```python
import jax
import jax.numpy as jnp
from jax import lax
from jax.experimental import pallas as pl
from jax.experimental.pallas import tpu as pltpu
from jax.sharding import PartitionSpec as P

HEADS = 32
LAT = 512
NOPE = 128
ROPE = 64
VDIM = 128
BLOCK = 128
STEPS = 2
D = 7168
LEN = 384
YS = 4
ZS = 4
TP = YS * ZS
REPS = 16
ROWS_DEV = 16
COLS = D // YS
EPSILON = 1e-06
SCALING = (NOPE + ROPE) ** (-0.5)
MESH = pl.DeviceIdType.MESH
BF = jnp.bfloat16
F32 = jnp.float32
VM = pl.BlockSpec(memory_space=pltpu.VMEM)
SM = pl.BlockSpec(memory_space=pltpu.SMEM)
ANY = pl.BlockSpec(memory_space=pl.ANY)


def rem(a, b):
    return lax.rem(a, jnp.int32(b))


def div(a, b):
    return lax.div(a, jnp.int32(b))


def rcopy(src, dst, send_sem, recv_sem, **where):
    return pltpu.make_async_remote_copy(
        src_ref=src,
        dst_ref=dst,
        send_sem=send_sem,
        recv_sem=recv_sem,
        device_id=where,
        device_id_type=MESH,
    )


def greet(tp_peers, rep_peers):
    barrier = pltpu.get_barrier_semaphore()
    for t in tp_peers:
        pl.semaphore_signal(barrier, inc=1, device_id={"tp": t}, device_id_type=MESH)
    for r in rep_peers:
        pl.semaphore_signal(barrier, inc=1, device_id={"rep": r}, device_id_type=MESH)
    pl.semaphore_wait(barrier, len(tp_peers) + len(rep_peers))


def mm(a, b, contract=((1,), (0,))):
    return lax.dot_general(a, b, (contract, ((), ())), preferred_element_type=F32)


def push_kernel(
    slot_ref,
    bver_ref,
    rver_ref,
    oscale_ref,
    tw_ref,
    ow_ref,
    sw_ref,
    ss_ref,
    dq_ref,
    gath,
    sel,
    buck,
    gsend,
    grecv,
    tsend,
    trecv,
    csend,
    crecv,
):
    rep, tp = lax.axis_index("rep"), lax.axis_index("tp")
    zh, x, c = div(rep, 8), rem(div(rep, 2), 4), rem(rep, 2)
    zpeer = rem(rep + 8, 16)
    cpeer = rep + 1 - 2 * c
    xpeers = [zh * 8 + rem(x + dx, 4) * 2 + c for dx in (1, 2, 3)]
    greet([rem(tp + k, TP) for k in range(1, TP)], [zpeer, cpeer] + xpeers)

    def block(b):
        return gath.at[pl.ds(2 * b, 2)]

    sent = []

    def send(src, b, to):
        copy = rcopy(src, block(b), gsend.at[len(sent)], grecv.at[b], rep=to)
        copy.start()
        sent.append(copy)

    def arrived(b):
        rcopy(block(b), block(b), gsend.at[0], grecv.at[b], rep=zpeer).wait_recv()

    for to in [zpeer] + xpeers + [cpeer]:
        send(tw_ref, rep, to)
    gath[pl.ds(2 * rep, 2)] = tw_ref[...]
    arrived(zpeer)
    for to in xpeers + [cpeer]:
        send(block(zpeer), zpeer, to)
    for xp in xpeers:
        arrived(xp)
        send(block(xp), xp, cpeer)
    for xp in xpeers:
        b = rem(xp + 8, 16)
        arrived(b)
        send(block(b), b, cpeer)
    for b in [cpeer, rem(cpeer + 8, 16)]:
        arrived(b)
    for xp in xpeers:
        other = xp + 1 - 2 * c
        arrived(other)
        arrived(rem(other + 8, 16))

    def part(src):
        return buck.at[c, pl.ds(pl.multiple_of(32 * src, 32), 32), :]

    def out_copy(k):
        t = rem(tp + k, TP)
        return rcopy(sel.at[k], part(tp), tsend.at[k], trecv.at[tp], tp=t)

    def pick(k, carry):
        t = rem(tp + k, TP)
        sel[k] = gath[slot_ref[2 * t + c]]
        out_copy(k).start()
        return carry

    lax.fori_loop(1, TP, pick, 0)
    buck[c, pl.ds(pl.multiple_of(32 * tp, 32), 32), :] = gath[slot_ref[2 * tp + c]]

    def take(k, carry):
        src = rem(tp + TP - k, TP)
        rcopy(part(src), part(src), tsend.at[k], trecv.at[src], tp=src).wait_recv()
        return carry

    lax.fori_loop(1, TP, take, 0)
    swap = rcopy(buck.at[c], buck.at[c], csend, crecv, rep=cpeer)
    swap.start()
    rcopy(buck.at[1 - c], buck.at[1 - c], csend, crecv, rep=cpeer).wait_recv()

    cell_row = lax.broadcasted_iota(jnp.int32, (4, 4), 0)
    cell_col = lax.broadcasted_iota(jnp.int32, (4, 4), 1)
    scales = jnp.zeros((4, 4), F32)
    for hh in range(2):
        head = 2 * tp + hh
        stale = (rver_ref[0, head] != bver_ref[head]).astype(jnp.int32)
        for i in range(4):
            for cc in range(2):
                rows = slice(i * BLOCK, (i + 1) * BLOCK)
                col = hh * 256 + cc * BLOCK
                raw = buck[hh, rows, cc * BLOCK : (cc + 1) * BLOCK].astype(F32)
                peak = jnp.max(jnp.abs(raw), axis=0, keepdims=True)
                peak = jnp.max(peak, axis=1, keepdims=True)
                scale = peak + EPSILON
                fresh = (raw / scale).astype(BF).astype(F32)
                old = ow_ref[0, rows, col : col + BLOCK].astype(F32)
                served = jnp.where(jnp.zeros((BLOCK, BLOCK), jnp.int32) + stale != 0, fresh, old)
                held = jnp.zeros((1, 1), F32) + oscale_ref[0, i, 2 * hh + cc]
                used = jnp.where(jnp.zeros((1, 1), jnp.int32) + stale != 0, scale, held)
                sw_ref[0, rows, col : col + BLOCK] = served.astype(BF)
                dq_ref[rows, col : col + BLOCK] = (served * used).astype(BF)
                here = (cell_row == i) & (cell_col == 2 * hh + cc)
                scales = jnp.where(here, used, scales)
    ss_ref[0] = scales

    for copy in sent:
        copy.wait_send()

    def drain(k, carry):
        out_copy(k).wait_send()
        return carry

    lax.fori_loop(1, TP, drain, 0)
    swap.wait_send()


def push(trainer_weight, bucket_slot, bucket_version, replica_version, old_weight, old_scale):
    dma = pltpu.SemaphoreType.DMA
    return pl.pallas_call(
        push_kernel,
        out_shape=(
            jax.ShapeDtypeStruct((1, LAT, 512), BF),
            jax.ShapeDtypeStruct((1, 4, 4), F32),
            jax.ShapeDtypeStruct((LAT, 512), BF),
        ),
        in_specs=[SM, SM, SM, SM, VM, VM],
        out_specs=(VM, VM, VM),
        scratch_shapes=[
            pltpu.VMEM((HEADS, 32, 256), BF),
            pltpu.VMEM((TP, 32, 256), BF),
            pltpu.VMEM((2, LAT, 256), BF),
            dma((15,)),
            dma((REPS,)),
            dma((TP,)),
            dma((TP,)),
            dma(()),
            dma(()),
        ],
        compiler_params=pltpu.CompilerParams(
            collective_id=0, has_side_effects=True, vmem_limit_bytes=24 * 2**20
        ),
        name="push",
    )(bucket_slot, bucket_version, replica_version, old_scale, trainer_weight, old_weight)


def attend_kernel(
    len_ref,
    dq_ref,
    qn_ref,
    qp_ref,
    rope_ref,
    tok_ref,
    cache_hbm,
    weight_hbm,
    ho_ref,
    wp,
    cache,
    perm,
    ropes,
    kr,
    toks,
    qs,
    qr,
    qrr,
    qrow,
    qro,
    attr,
    ab,
    ar,
    lsem,
    wsend,
    wrecv,
    xsend,
    xrecv,
    psend,
    precv,
    qsend,
    qrecv,
    asend,
    arecv,
):
    rep, tp = lax.axis_index("rep"), lax.axis_index("tp")
    y, z, c = div(tp, ZS), rem(tp, ZS), rem(rep, 2)
    cpeer = rep + 1 - 2 * c

    load = pltpu.make_async_copy(cache_hbm.at[0], cache, lsem.at[0])
    load.start()
    own_w = pltpu.make_async_copy(
        weight_hbm.at[:, pl.ds(pl.multiple_of(COLS * y, 256), COLS)], wp.at[y], lsem.at[1]
    )
    own_w.start()
    greet([rem(tp + k, TP) for k in range(1, TP)], [cpeer])

    def half(yy, side):
        return wp.at[yy, pl.ds(pl.multiple_of(128 * side, 128), 128), :]

    def rows16(t):
        return pl.ds(pl.multiple_of(16 * t, 16), 16)

    def rope_copy(k):
        t = rem(tp + k, TP)
        return rcopy(qp_ref.at[:, 0, rows16(t), :], qrr.at[:, tp], psend.at[k], precv.at[tp], tp=t)

    def query_copy(s, k):
        t = rem(tp + k, TP)
        return rcopy(
            qs.at[s, :, rows16(t), :], qr.at[s, :, tp], qsend.at[s, k], qrecv.at[s, tp], tp=t
        )

    def back_copy(s, k):
        t = rem(tp + k, TP)
        return rcopy(
            ab.at[s, :, t], ar.at[s, :, rows16(tp), :], asend.at[s, k], arecv.at[s, tp], tp=t
        )

    def weight_copy(dy):
        to = rem(y + dy, YS)
        src = weight_hbm.at[
            pl.ds(pl.multiple_of(128 * c, 128), 128), pl.ds(pl.multiple_of(COLS * to, 256), COLS)
        ]
        return rcopy(src, half(y, c), wsend.at[dy], wrecv.at[y], tp=to * ZS + z)

    def swap_copy(dy):
        src = rem(y + YS - dy, YS)
        return rcopy(half(src, c), half(src, c), xsend.at[dy], xrecv.at[src], rep=cpeer)

    def each(first, fn):
        def body(k, carry):
            fn(k)
            return carry

        lax.fori_loop(first, TP, body, 0)

    each(1, lambda k: rope_copy(k).start())
    for s in range(STEPS):
        for hh in range(2):
            qs[s, hh] = mm(
                qn_ref[s, 0, :, hh * NOPE : (hh + 1) * NOPE],
                dq_ref[:, hh * 256 : hh * 256 + NOPE],
                ((1,), (1,)),
            ).astype(BF)
        each(1, lambda k: query_copy(s, k).start())
    for dy in (1, 2, 3):
        weight_copy(dy).start()

    pi = lax.broadcasted_iota(jnp.int32, (256, 256), 0)
    pj = lax.broadcasted_iota(jnp.int32, (256, 256), 1)
    swapped = ((pi >> 4) == (pj & 15)) & ((pi & 15) == (pj >> 4))
    perm[...] = jnp.where(swapped, 1.0, 0.0).astype(BF)
    toks[...] = jnp.zeros_like(toks)
    toks[:, :, 0 : LAT + ROPE] = tok_ref[:, 0].astype(F32)
    for s in range(STEPS):
        qrr[s, tp] = qp_ref[s, 0, rows16(tp), :]
        for hh in range(2):
            qr[s, hh, tp] = qs[s, hh, rows16(tp), :]

    for g in range(12):
        tiles = [rope_ref[0, :, (16 * g + i) * 128 : (16 * g + i + 1) * 128] for i in range(16)]
        turned = mm(perm[...], jnp.concatenate(tiles, axis=0)).astype(BF)
        ropes[:, 16 * g : 16 * (g + 1), :] = turned.reshape(16, 16, 128)
    si = lax.broadcasted_iota(jnp.int32, (LEN, LEN // 2), 0)
    sj = lax.broadcasted_iota(jnp.int32, (LEN, LEN // 2), 1)
    spread = jnp.where((si >> 1) == sj, 1.0, 0.0).astype(BF)
    ki = lax.broadcasted_iota(jnp.int32, (LEN, 128), 0)
    kj = lax.broadcasted_iota(jnp.int32, (LEN, 128), 1)
    kept = (ki & 1) == (kj >> 6)

    def place(r, carry):
        kr[r] = jnp.where(kept, mm(spread, ropes[r]), 0.0).astype(BF)
        return carry

    lax.fori_loop(0, ROWS_DEV, place, 0)
    load.wait()

    di = lax.broadcasted_iota(jnp.int32, (128, 256), 0)
    dj = lax.broadcasted_iota(jnp.int32, (128, 256), 1)
    double = jnp.where(di == (dj >> 7) * 64 + (dj & 63), 1.0, 0.0).astype(BF)
    position = lax.broadcasted_iota(jnp.int32, (1, LEN), 1)

    def got_rope(k):
        src = rem(tp + TP - k, TP)
        rcopy(qrr.at[:, src], qrr.at[:, src], psend.at[k], precv.at[src], tp=src).wait_recv()

    each(1, got_rope)

    for s in range(STEPS):

        def got_query(k):
            src = rem(tp + TP - k, TP)
            there = qr.at[s, :, src]
            rcopy(there, there, qsend.at[s, k], qrecv.at[s, src], tp=src).wait_recv()

        each(1, got_query)
        for hh in range(2):
            turned = mm(perm[...], qr[s, hh].reshape(256, LAT)).astype(BF)
            qrow[:, 16 * hh : 16 * (hh + 1), :] = turned.reshape(16, 16, LAT)
        turned = mm(perm[...], qrr[s].reshape(256, 128)).astype(BF)
        turned = mm(turned, double).astype(BF)
        for hh in range(2):
            qro[:, 16 * hh : 16 * (hh + 1), :] = turned[:, 128 * hh : 128 * (hh + 1)].reshape(
                16, 16, 128
            )

        def attend_row(r, carry):
            q_lat, q_rope, keys = qrow[r], qro[r], cache[r]
            score = mm(q_lat, keys, ((1,), (1,))) + mm(q_rope, kr[r], ((1,), (1,)))
            score = jnp.where(position < len_ref[0, r], score * SCALING, -jnp.inf)
            top = jnp.max(score, axis=1, keepdims=True)
            lat32, rope32 = q_lat.astype(F32), q_rope.astype(F32)
            news = []
            for t in range(s + 1):
                tok = toks[t, pl.ds(r, 1), :]
                new = jnp.sum(lat32 * tok[:, :LAT], axis=1, keepdims=True)
                new = new + jnp.sum(rope32 * tok[:, LAT:], axis=1, keepdims=True)
                news.append((new * SCALING, tok[:, :LAT]))
            for new, _ in news:
                top = jnp.maximum(top, new)
            expped = jnp.exp(score - top)
            new_exp = [jnp.exp(new - top) for new, _ in news]
            total = jnp.sum(expped, axis=1, keepdims=True)
            for e in new_exp:
                total = total + e
            inverse = 1.0 / total
            out = mm((expped * inverse).astype(BF), keys)
            for e, (_, tok) in zip(new_exp, news):
                out = out + (e * inverse).astype(BF).astype(F32) * tok
            out = out.astype(BF)
            attr[0, r] = out[:16]
            attr[1, r] = out[16:]
            return carry

        lax.fori_loop(0, ROWS_DEV, attend_row, 0, unroll=4)
        for hh in range(2):
            turned = mm(perm[...], attr[hh].reshape(256, LAT)).astype(BF)
            ab[s, hh] = turned.reshape(16, 16, LAT)
        each(1, lambda k: back_copy(s, k).start())
        for hh in range(2):
            ar[s, hh, rows16(tp), :] = ab[s, hh, tp]

    for dy in (1, 2, 3):
        src = rem(y + YS - dy, YS)
        there = half(src, c)
        rcopy(there, there, wsend.at[dy], wrecv.at[src], tp=src * ZS + z).wait_recv()
        swap_copy(dy).start()

    for s in range(STEPS):

        def got_back(k):
            src = rem(tp + TP - k, TP)
            there = ar.at[s, :, rows16(src), :]
            rcopy(there, there, asend.at[s, k], arecv.at[s, src], tp=src).wait_recv()

        each(1, got_back)
        for hh in range(2):
            ho_ref[s, :, hh * VDIM : (hh + 1) * VDIM] = mm(
                ar[s, hh], dq_ref[:, hh * 256 + NOPE : (hh + 1) * 256]
            ).astype(BF)

    own_w.wait()
    for dy in (1, 2, 3):
        src = rem(y + YS - dy, YS)
        there = half(src, 1 - c)
        rcopy(there, there, xsend.at[dy], xrecv.at[src], rep=cpeer).wait_recv()
    for dy in (1, 2, 3):
        weight_copy(dy).wait_send()
        swap_copy(dy).wait_send()
    each(1, lambda k: rope_copy(k).wait_send())
    for s in range(STEPS):
        each(1, lambda k: query_copy(s, k).wait_send())
        each(1, lambda k: back_copy(s, k).wait_send())


def attend(dq, q_nope, q_rope, cache_latent, cache_rope, new_token, lengths, out_weight):
    dma = pltpu.SemaphoreType.DMA
    return pl.pallas_call(
        attend_kernel,
        out_shape=(
            jax.ShapeDtypeStruct((STEPS, 256, 256), BF),
            jax.ShapeDtypeStruct((YS, 256, COLS), BF),
        ),
        in_specs=[SM, VM, VM, VM, VM, VM, ANY, ANY],
        out_specs=(VM, VM),
        scratch_shapes=[
            pltpu.VMEM((ROWS_DEV, LEN, LAT), BF),
            pltpu.VMEM((256, 256), BF),
            pltpu.VMEM((ROWS_DEV, LEN // 2, 128), BF),
            pltpu.VMEM((ROWS_DEV, LEN, 128), BF),
            pltpu.VMEM((STEPS, ROWS_DEV, 640), F32),
            pltpu.VMEM((STEPS, 2, 256, LAT), BF),
            pltpu.VMEM((STEPS, 2, TP, 16, LAT), BF),
            pltpu.VMEM((STEPS, TP, 16, 128), BF),
            pltpu.VMEM((ROWS_DEV, HEADS, LAT), BF),
            pltpu.VMEM((ROWS_DEV, HEADS, 128), BF),
            pltpu.VMEM((2, ROWS_DEV, 16, LAT), BF),
            pltpu.VMEM((STEPS, 2, TP, 16, LAT), BF),
            pltpu.VMEM((STEPS, 2, 256, LAT), BF),
            dma((2,)),
            dma((YS,)),
            dma((YS,)),
            dma((YS,)),
            dma((YS,)),
            dma((TP,)),
            dma((TP,)),
            dma((STEPS, TP)),
            dma((STEPS, TP)),
            dma((STEPS, TP)),
            dma((STEPS, TP)),
        ],
        compiler_params=pltpu.CompilerParams(
            collective_id=1, has_side_effects=True, vmem_limit_bytes=48 * 2**20
        ),
        name="attend",
    )(lengths, dq, q_nope, q_rope, cache_rope, new_token, cache_latent, out_weight)


def project_kernel(
    ho_ref, wp, dec, hg, pb, r1, r2, sx, fin, hsend, hrecv, s1send, s1recv, s2send, s2recv, fsend, frecv
):
    tp = lax.axis_index("tp")
    y, z = div(tp, ZS), rem(tp, ZS)
    near = z + 1 - 2 * rem(z, 2)
    far = rem(z + 2, ZS)
    mirror = 3 - z
    peers = [rem(y + dy, YS) * ZS + z for dy in (1, 2, 3)]
    greet(peers + [y * ZS + near, y * ZS + far], [])

    def gather_copy(s, dy):
        to = rem(y + dy, YS) * ZS + z
        return rcopy(ho_ref.at[s], hg.at[s, y], hsend.at[s, dy], hrecv.at[s, y], tp=to)

    def near_copy(s, which):
        blk = mirror if which == 0 else near
        return rcopy(
            pb.at[s, :, blk], r1.at[s, which], s1send.at[s, which], s1recv.at[s, which], tp=y * ZS + near
        )

    def far_copy(s):
        return rcopy(sx.at[s], r2.at[s], s2send.at[s], s2recv.at[s], tp=y * ZS + far)

    def home_copy(s, dy):
        to = rem(y + dy, YS)
        there = dec.at[s, 0, :, pl.ds(pl.multiple_of(COLS * y, 256), COLS)]
        return rcopy(fin.at[s, to], there, fsend.at[s, dy], frecv.at[s, y], tp=to * ZS + z)

    for s in range(STEPS):
        for dy in (1, 2, 3):
            gather_copy(s, dy).start()
        hg[s, y] = ho_ref[s]

    for s in range(STEPS):
        for dy in (1, 2, 3):
            src = rem(y + YS - dy, YS)
            there = hg.at[s, src]
            rcopy(there, there, hsend.at[s, dy], hrecv.at[s, src], tp=src * ZS + z).wait_recv()

        def columns(n, carry):
            cols = pl.ds(pl.multiple_of(256 * n, 256), 256)
            total = mm(hg[s, 0], wp[0, :, cols])
            for k in range(1, YS):
                total = total + mm(hg[s, k], wp[k, :, cols])
            pb[s, :, :, :, cols] = total.astype(BF).reshape(YS, ZS, 16, 256)
            return carry

        lax.fori_loop(0, COLS // 256, columns, 0)
        for which in range(2):
            near_copy(s, which).start()

    for s in range(STEPS):
        near_copy(s, 0).wait_recv()
        sx[s] = (pb[s, :, far].astype(F32) + r1[s, 0].astype(F32)).astype(BF)
        far_copy(s).start()

    for s in range(STEPS):
        near_copy(s, 1).wait_recv()
        far_copy(s).wait_recv()
        fin[s] = (
            pb[s, :, z].astype(F32) + r1[s, 1].astype(F32) + r2[s].astype(F32)
        ).astype(BF)
        for dy in (1, 2, 3):
            home_copy(s, dy).start()
        dec[s, 0, :, pl.ds(pl.multiple_of(COLS * y, 256), COLS)] = fin[s, y]

    for s in range(STEPS):
        for dy in (1, 2, 3):
            src = rem(y + YS - dy, YS)
            there = dec.at[s, 0, :, pl.ds(pl.multiple_of(COLS * src, 256), COLS)]
            rcopy(there, there, fsend.at[s, dy], frecv.at[s, src], tp=src * ZS + z).wait_recv()
    for s in range(STEPS):
        for dy in (1, 2, 3):
            gather_copy(s, dy).wait_send()
            home_copy(s, dy).wait_send()
        for which in range(2):
            near_copy(s, which).wait_send()
        far_copy(s).wait_send()


def project(ho, wp):
    dma = pltpu.SemaphoreType.DMA
    block = (STEPS, YS, 16, COLS)
    return pl.pallas_call(
        project_kernel,
        out_shape=jax.ShapeDtypeStruct((STEPS, 1, 16, D), BF),
        in_specs=[VM, VM],
        out_specs=VM,
        scratch_shapes=[
            pltpu.VMEM((STEPS, YS, 256, 256), BF),
            pltpu.VMEM((STEPS, YS, ZS, 16, COLS), BF),
            pltpu.VMEM((STEPS, 2, YS, 16, COLS), BF),
            pltpu.VMEM(block, BF),
            pltpu.VMEM(block, BF),
            pltpu.VMEM(block, BF),
            dma((STEPS, YS)),
            dma((STEPS, YS)),
            dma((STEPS, 2)),
            dma((STEPS, 2)),
            dma((STEPS,)),
            dma((STEPS,)),
            dma((STEPS, YS)),
            dma((STEPS, YS)),
        ],
        compiler_params=pltpu.CompilerParams(
            collective_id=2, has_side_effects=True, vmem_limit_bytes=40 * 2**20
        ),
        name="project",
    )(ho, wp)


def local(
    trainer_weight,
    bucket_slot,
    bucket_version,
    replica_version,
    old_weight,
    old_scale,
    q_nope,
    q_rope,
    cache_latent,
    cache_rope,
    new_token,
    lengths,
    out_weight,
):
    served_weight, served_scale, dq = push(
        trainer_weight, bucket_slot, bucket_version, replica_version, old_weight, old_scale
    )
    ho, wp = attend(
        dq, q_nope, q_rope, cache_latent, cache_rope, new_token, lengths, out_weight
    )
    decoded = project(ho, wp)
    return (served_weight, served_scale, decoded)


def solution(mesh):
    return jax.shard_map(
        local,
        mesh=mesh,
        in_specs=(
            P("rep", "tp", None),
            P(),
            P(),
            P("rep", None),
            P("rep", None, "tp"),
            P("rep", None, "tp"),
            P(None, "rep", None, "tp"),
            P(None, "rep", None, "tp"),
            P("rep", "tp", None, None),
            P("rep", "tp", None),
            P(None, "rep", "tp", None),
            P("rep", "tp"),
            P("tp", None),
        ),
        out_specs=(P("rep", None, "tp"), P("rep", None, "tp"), P(None, "rep", "tp", None)),
        check_vma=False,
    )
```

```python
import jax
import jax.numpy as jnp
from jax import lax
from jax.experimental import pallas as pl
from jax.experimental.pallas import tpu as pltpu
from jax.sharding import PartitionSpec as P

HEADS = 32
LAT = 512
NOPE = 128
ROPE = 64
VDIM = 128
BLOCK = 128
STEPS = 2
D = 7168
LEN = 384
YS = 4
ZS = 4
TP = YS * ZS
REPS = 16
ROWS_DEV = 16
COLS = D // YS
HALF = COLS // 2
CHUNKS = 4
EPSILON = 1e-06
SCALING = (NOPE + ROPE) ** (-0.5)
MESH = pl.DeviceIdType.MESH
BF = jnp.bfloat16
F32 = jnp.float32
VM = pl.BlockSpec(memory_space=pltpu.VMEM)
SM = pl.BlockSpec(memory_space=pltpu.SMEM)
ANY = pl.BlockSpec(memory_space=pl.ANY)


def rem(a, b):
    return lax.rem(a, jnp.int32(b))


def div(a, b):
    return lax.div(a, jnp.int32(b))


def rcopy(src, dst, send_sem, recv_sem, **where):
    return pltpu.make_async_remote_copy(
        src_ref=src,
        dst_ref=dst,
        send_sem=send_sem,
        recv_sem=recv_sem,
        device_id=where,
        device_id_type=MESH,
    )


def greet(tp_peers, rep_peers):
    barrier = pltpu.get_barrier_semaphore()
    for t in tp_peers:
        pl.semaphore_signal(barrier, inc=1, device_id={"tp": t}, device_id_type=MESH)
    for r in rep_peers:
        pl.semaphore_signal(barrier, inc=1, device_id={"rep": r}, device_id_type=MESH)
    pl.semaphore_wait(barrier, len(tp_peers) + len(rep_peers))


def mm(a, b, contract=((1,), (0,))):
    return lax.dot_general(a, b, (contract, ((), ())), preferred_element_type=F32)


def everything(
    slot_ref,
    bver_ref,
    rver_ref,
    oscale_ref,
    len_ref,
    tw_hbm,
    ow_hbm,
    qn_hbm,
    qp_hbm,
    cache_hbm,
    rope_hbm,
    tok_hbm,
    weight_hbm,
    sw_ref,
    ss_ref,
    dec,
    gath,
    sel,
    buck,
    ow,
    dq,
    qn,
    rope,
    tok,
    cache,
    wp,
    perm,
    ropes,
    kr,
    toks,
    qs,
    qr,
    qrr,
    qrow,
    qro,
    attr,
    ab,
    ar,
    ho,
    hg,
    pb,
    r1,
    r2,
    sx,
    fin,
    lsem,
    gsend,
    grecv,
    tsend,
    trecv,
    csend,
    crecv,
    wsend,
    wrecv,
    xsend,
    xrecv,
    psend,
    precv,
    qsend,
    qrecv,
    asend,
    arecv,
    hsend,
    hrecv,
    s1send,
    s1recv,
    s2send,
    s2recv,
    fsend,
    frecv,
):
    rep, tp = lax.axis_index("rep"), lax.axis_index("tp")
    zh, x, c = div(rep, 8), rem(div(rep, 2), 4), rem(rep, 2)
    y, z = div(tp, ZS), rem(tp, ZS)
    zpeer = rem(rep + 8, 16)
    cpeer = rep + 1 - 2 * c
    xpeers = [zh * 8 + rem(x + dx, 4) * 2 + c for dx in (1, 2, 3)]
    near = z + 1 - 2 * rem(z, 2)
    far = rem(z + 2, ZS)
    mirror = 3 - z

    def rows16(t):
        return pl.ds(pl.multiple_of(16 * t, 16), 16)

    def rows32(t):
        return pl.ds(pl.multiple_of(32 * t, 32), 32)

    def columns(yy):
        return pl.ds(pl.multiple_of(COLS * yy, 256), COLS)

    def each(fn):
        def body(k, carry):
            fn(k)
            return carry

        lax.fori_loop(1, TP, body, 0)

    def source(k):
        return rem(tp + TP - k, TP)

    loads = [
        pltpu.make_async_copy(src, dst, lsem.at[i])
        for i, (src, dst) in enumerate(
            [
                (tw_hbm, gath.at[pl.ds(2 * rep, 2)]),
                (qp_hbm.at[:, 0, rows16(tp), :], qrr.at[:, tp]),
                (tok_hbm.at[:, 0], tok),
                (rope_hbm.at[0], rope),
                (ow_hbm.at[0], ow),
                (qn_hbm.at[:, 0], qn),
                (cache_hbm.at[0], cache),
                (weight_hbm.at[:, columns(y)], wp.at[y]),
            ]
        )
    ]
    load_tw, load_qp, load_tok, load_rope, load_ow, load_qn, load_cache, load_w = loads
    for copy in loads:
        copy.start()
    greet([rem(tp + k, TP) for k in range(1, TP)], [zpeer, cpeer] + xpeers)

    def block(b):
        return gath.at[pl.ds(2 * b, 2)]

    sent = []

    def pass_on(src, b, to):
        copy = rcopy(src, block(b), gsend.at[len(sent)], grecv.at[b], rep=to)
        copy.start()
        sent.append(copy)

    def arrived(b):
        rcopy(block(b), block(b), gsend.at[0], grecv.at[b], rep=zpeer).wait_recv()

    def part(src):
        return buck.at[c, rows32(src), :]

    def pick_copy(k):
        t = rem(tp + k, TP)
        return rcopy(sel.at[k], part(tp), tsend.at[k], trecv.at[tp], tp=t)

    def half(yy, side):
        return wp.at[yy, pl.ds(pl.multiple_of(128 * side, 128), 128), :]

    def weight_copy(dy):
        to = rem(y + dy, YS)
        src = weight_hbm.at[pl.ds(pl.multiple_of(128 * c, 128), 128), columns(to)]
        return rcopy(src, half(y, c), wsend.at[dy], wrecv.at[y], tp=to * ZS + z)

    def swap_copy(dy):
        src = rem(y + YS - dy, YS)
        return rcopy(half(src, c), half(src, c), xsend.at[dy], xrecv.at[src], rep=cpeer)

    def rope_copy(k):
        t = rem(tp + k, TP)
        return rcopy(qp_hbm.at[:, 0, rows16(t), :], qrr.at[:, tp], psend.at[k], precv.at[tp], tp=t)

    def query_copy(s, k):
        t = rem(tp + k, TP)
        return rcopy(
            qs.at[s, :, rows16(t), :], qr.at[s, :, tp], qsend.at[s, k], qrecv.at[s, tp], tp=t
        )

    def back_copy(s, k):
        t = rem(tp + k, TP)
        return rcopy(
            ab.at[s, :, t], ar.at[s, :, rows16(tp), :], asend.at[s, k], arecv.at[s, tp], tp=t
        )

    def gather_copy(s, dy):
        to = rem(y + dy, YS) * ZS + z
        return rcopy(ho.at[s], hg.at[s, y], hsend.at[s, dy], hrecv.at[s, y], tp=to)

    def near_copy(q, which):
        blk = mirror if which == 0 else near
        return rcopy(
            pb.at[q, :, blk], r1.at[q, which], s1send.at[q, which], s1recv.at[q, which], tp=y * ZS + near
        )

    def far_copy(q):
        return rcopy(sx.at[q], r2.at[q], s2send.at[q], s2recv.at[q], tp=y * ZS + far)

    def home(q, yy):
        first = pl.multiple_of(COLS * yy + HALF * (q % 2), 128)
        return dec.at[q // 2, 0, :, pl.ds(first, HALF)]

    def home_copy(q, dy):
        to = rem(y + dy, YS)
        return rcopy(fin.at[q, to], home(q, y), fsend.at[q, dy], frecv.at[q, y], tp=to * ZS + z)

    for to in [zpeer] + xpeers + [cpeer]:
        pass_on(tw_hbm, rep, to)
    weight_copy(1).start()
    weight_copy(3).start()
    arrived(zpeer)
    for to in xpeers + [cpeer]:
        pass_on(block(zpeer), zpeer, to)
    for xp in xpeers:
        arrived(xp)
        pass_on(block(xp), xp, cpeer)
    for xp in xpeers:
        b = rem(xp + 8, 16)
        arrived(b)
        pass_on(block(b), b, cpeer)
    load_tw.wait()
    for b in [cpeer, rem(cpeer + 8, 16)]:
        arrived(b)
    for xp in xpeers:
        other = xp + 1 - 2 * c
        arrived(other)
        arrived(rem(other + 8, 16))

    def pick(k):
        sel[k] = gath[slot_ref[2 * rem(tp + k, TP) + c]]
        pick_copy(k).start()

    each(pick)
    buck[c, rows32(tp), :] = gath[slot_ref[2 * tp + c]]
    each(lambda k: rope_copy(k).start())
    weight_copy(2).start()

    pi = lax.broadcasted_iota(jnp.int32, (256, 256), 0)
    pj = lax.broadcasted_iota(jnp.int32, (256, 256), 1)
    swapped = ((pi >> 4) == (pj & 15)) & ((pi & 15) == (pj >> 4))
    perm[...] = jnp.where(swapped, 1.0, 0.0).astype(BF)
    load_tok.wait()
    toks[...] = jnp.zeros_like(toks)
    toks[:, :, 0 : LAT + ROPE] = tok[...].astype(F32)
    load_rope.wait()
    for g in range(12):
        tiles = [rope[:, (16 * g + i) * 128 : (16 * g + i + 1) * 128] for i in range(16)]
        turned = mm(perm[...], jnp.concatenate(tiles, axis=0)).astype(BF)
        ropes[:, 16 * g : 16 * (g + 1), :] = turned.reshape(16, 16, 128)

    def bucket_arrived(k):
        src = source(k)
        rcopy(part(src), part(src), tsend.at[k], trecv.at[src], tp=src).wait_recv()

    each(bucket_arrived)
    swap = rcopy(buck.at[c], buck.at[c], csend, crecv, rep=cpeer)
    swap.start()
    load_ow.wait()
    load_qn.wait()
    rcopy(buck.at[1 - c], buck.at[1 - c], csend, crecv, rep=cpeer).wait_recv()

    cell_row = lax.broadcasted_iota(jnp.int32, (4, 4), 0)
    cell_col = lax.broadcasted_iota(jnp.int32, (4, 4), 1)

    def serve(hh, cc, scales):
        head = 2 * tp + hh
        stale = (rver_ref[0, head] != bver_ref[head]).astype(jnp.int32)
        col = hh * 256 + cc * BLOCK
        for i in range(4):
            rows = slice(i * BLOCK, (i + 1) * BLOCK)
            raw = buck[hh, rows, cc * BLOCK : (cc + 1) * BLOCK].astype(F32)
            peak = jnp.max(jnp.abs(raw), axis=0, keepdims=True)
            peak = jnp.max(peak, axis=1, keepdims=True)
            scale = peak + EPSILON
            fresh = (raw / scale).astype(BF).astype(F32)
            old = ow[rows, col : col + BLOCK].astype(F32)
            served = jnp.where(jnp.zeros((BLOCK, BLOCK), jnp.int32) + stale != 0, fresh, old)
            held = jnp.zeros((1, 1), F32) + oscale_ref[0, i, 2 * hh + cc]
            used = jnp.where(jnp.zeros((1, 1), jnp.int32) + stale != 0, scale, held)
            sw_ref[0, rows, col : col + BLOCK] = served.astype(BF)
            dq[rows, col : col + BLOCK] = (served * used).astype(BF)
            here = (cell_row == i) & (cell_col == 2 * hh + cc)
            scales = jnp.where(here, used, scales)
        return scales

    scales = jnp.zeros((4, 4), F32)
    for hh in range(2):
        scales = serve(hh, 0, scales)

    for s in range(STEPS):
        for hh in range(2):
            qs[s, hh] = mm(
                qn[s, :, hh * NOPE : (hh + 1) * NOPE],
                dq[:, hh * 256 : hh * 256 + NOPE],
                ((1,), (1,)),
            ).astype(BF)
        each(lambda k: query_copy(s, k).start())
    for hh in range(2):
        scales = serve(hh, 1, scales)
    ss_ref[0] = scales
    for s in range(STEPS):
        for hh in range(2):
            qr[s, hh, tp] = qs[s, hh, rows16(tp), :]

    si = lax.broadcasted_iota(jnp.int32, (LEN, LEN // 2), 0)
    sj = lax.broadcasted_iota(jnp.int32, (LEN, LEN // 2), 1)
    spread = jnp.where((si >> 1) == sj, 1.0, 0.0).astype(BF)
    ki = lax.broadcasted_iota(jnp.int32, (LEN, 128), 0)
    kj = lax.broadcasted_iota(jnp.int32, (LEN, 128), 1)
    kept = (ki & 1) == (kj >> 6)

    def place(r, carry):
        kr[r] = jnp.where(kept, mm(spread, ropes[r]), 0.0).astype(BF)
        return carry

    lax.fori_loop(0, ROWS_DEV, place, 0)
    load_cache.wait()
    load_qp.wait()

    di = lax.broadcasted_iota(jnp.int32, (128, 256), 0)
    dj = lax.broadcasted_iota(jnp.int32, (128, 256), 1)
    double = jnp.where(di == (dj >> 7) * 64 + (dj & 63), 1.0, 0.0).astype(BF)
    position = lax.broadcasted_iota(jnp.int32, (1, LEN), 1)

    def rope_arrived(k):
        src = source(k)
        rcopy(qrr.at[:, src], qrr.at[:, src], psend.at[k], precv.at[src], tp=src).wait_recv()

    each(rope_arrived)

    for s in range(STEPS):

        def query_arrived(k):
            src = source(k)
            there = qr.at[s, :, src]
            rcopy(there, there, qsend.at[s, k], qrecv.at[s, src], tp=src).wait_recv()

        turned = mm(perm[...], qrr[s].reshape(256, 128)).astype(BF)
        turned = mm(turned, double).astype(BF)
        for hh in range(2):
            qro[:, 16 * hh : 16 * (hh + 1), :] = turned[:, 128 * hh : 128 * (hh + 1)].reshape(
                16, 16, 128
            )
        each(query_arrived)
        for hh in range(2):
            turned = mm(perm[...], qr[s, hh].reshape(256, LAT)).astype(BF)
            qrow[:, 16 * hh : 16 * (hh + 1), :] = turned.reshape(16, 16, LAT)

        def attend_row(r, carry):
            q_lat, q_rope, keys = qrow[r], qro[r], cache[r]
            score = mm(q_lat, keys, ((1,), (1,))) + mm(q_rope, kr[r], ((1,), (1,)))
            score = jnp.where(position < len_ref[0, r], score * SCALING, -jnp.inf)
            top = jnp.max(score, axis=1, keepdims=True)
            lat32, rope32 = q_lat.astype(F32), q_rope.astype(F32)
            news = []
            for t in range(s + 1):
                tok_r = toks[t, pl.ds(r, 1), :]
                new = jnp.sum(lat32 * tok_r[:, :LAT], axis=1, keepdims=True)
                new = new + jnp.sum(rope32 * tok_r[:, LAT:], axis=1, keepdims=True)
                news.append((new * SCALING, tok_r[:, :LAT]))
            for new, _ in news:
                top = jnp.maximum(top, new)
            expped = jnp.exp(score - top)
            new_exp = [jnp.exp(new - top) for new, _ in news]
            total = jnp.sum(expped, axis=1, keepdims=True)
            for e in new_exp:
                total = total + e
            inverse = 1.0 / total
            out = mm((expped * inverse).astype(BF), keys)
            for e, (_, tok_r) in zip(new_exp, news):
                out = out + (e * inverse).astype(BF).astype(F32) * tok_r
            out = out.astype(BF)
            attr[0, r] = out[:16]
            attr[1, r] = out[16:]
            return carry

        lax.fori_loop(0, ROWS_DEV, attend_row, 0, unroll=4)
        for hh in range(2):
            turned = mm(perm[...], attr[hh].reshape(256, LAT)).astype(BF)
            ab[s, hh] = turned.reshape(16, 16, LAT)
        each(lambda k: back_copy(s, k).start())
        for hh in range(2):
            ar[s, hh, rows16(tp), :] = ab[s, hh, tp]
        if s == 0:
            for dy in (1, 2, 3):
                src = rem(y + YS - dy, YS)
                there = half(src, c)
                rcopy(there, there, wsend.at[dy], wrecv.at[src], tp=src * ZS + z).wait_recv()
                swap_copy(dy).start()

    load_w.wait()
    for dy in (1, 2, 3):
        src = rem(y + YS - dy, YS)
        there = half(src, 1 - c)
        rcopy(there, there, xsend.at[dy], xrecv.at[src], rep=cpeer).wait_recv()

    def heads_out(s):
        def back_arrived(k):
            src = source(k)
            there = ar.at[s, :, rows16(src), :]
            rcopy(there, there, asend.at[s, k], arecv.at[s, src], tp=src).wait_recv()

        each(back_arrived)
        for hh in range(2):
            ho[s, :, hh * VDIM : (hh + 1) * VDIM] = mm(
                ar[s, hh], dq[:, hh * 256 + NOPE : (hh + 1) * 256]
            ).astype(BF)
        for dy in (1, 2, 3):
            gather_copy(s, dy).start()
        hg[s, y] = ho[s]

    def multiply(s):
        for dy in (1, 2, 3):
            src = rem(y + YS - dy, YS)
            there = hg.at[s, src]
            rcopy(there, there, hsend.at[s, dy], hrecv.at[s, src], tp=src * ZS + z).wait_recv()
        for q in (2 * s, 2 * s + 1):
            for first, width in ((0, 512), (512, 384)):
                cols = slice(HALF * (q % 2) + first, HALF * (q % 2) + first + width)
                total = mm(hg[s, 0], wp[0, :, cols])
                for k in range(1, YS):
                    total = total + mm(hg[s, k], wp[k, :, cols])
                pb[q, :, :, :, first : first + width] = total.astype(BF).reshape(YS, ZS, 16, width)
            for which in range(2):
                near_copy(q, which).start()

    def cross(q):
        near_copy(q, 0).wait_recv()
        sx[q] = (pb[q, :, far].astype(F32) + r1[q, 0].astype(F32)).astype(BF)
        far_copy(q).start()

    def finish(q):
        near_copy(q, 1).wait_recv()
        far_copy(q).wait_recv()
        fin[q] = (pb[q, :, z].astype(F32) + r1[q, 1].astype(F32) + r2[q].astype(F32)).astype(BF)
        for dy in (1, 2, 3):
            home_copy(q, dy).start()
        first = pl.multiple_of(COLS * y + HALF * (q % 2), 128)
        dec[q // 2, 0, :, pl.ds(first, HALF)] = fin[q, y]

    heads_out(0)
    multiply(0)
    heads_out(1)
    cross(0)
    multiply(1)
    cross(1)
    finish(0)
    cross(2)
    finish(1)
    cross(3)
    finish(2)
    finish(3)

    for q in range(CHUNKS):
        for dy in (1, 2, 3):
            src = rem(y + YS - dy, YS)
            rcopy(
                home(q, src), home(q, src), fsend.at[q, dy], frecv.at[q, src], tp=src * ZS + z
            ).wait_recv()

    for copy in sent:
        copy.wait_send()
    each(lambda k: pick_copy(k).wait_send())
    swap.wait_send()
    each(lambda k: rope_copy(k).wait_send())
    for dy in (1, 2, 3):
        weight_copy(dy).wait_send()
        swap_copy(dy).wait_send()
    for s in range(STEPS):
        each(lambda k: query_copy(s, k).wait_send())
        each(lambda k: back_copy(s, k).wait_send())
        for dy in (1, 2, 3):
            gather_copy(s, dy).wait_send()
    for q in range(CHUNKS):
        for which in range(2):
            near_copy(q, which).wait_send()
        far_copy(q).wait_send()
        for dy in (1, 2, 3):
            home_copy(q, dy).wait_send()


def local(
    trainer_weight,
    bucket_slot,
    bucket_version,
    replica_version,
    old_weight,
    old_scale,
    q_nope,
    q_rope,
    cache_latent,
    cache_rope,
    new_token,
    lengths,
    out_weight,
):
    dma = pltpu.SemaphoreType.DMA
    chunk = (CHUNKS, YS, 16, HALF)
    return pl.pallas_call(
        everything,
        out_shape=(
            jax.ShapeDtypeStruct((1, LAT, 512), BF),
            jax.ShapeDtypeStruct((1, 4, 4), F32),
            jax.ShapeDtypeStruct((STEPS, 1, 16, D), BF),
        ),
        in_specs=[SM] * 5 + [ANY] * 8,
        out_specs=(VM, VM, VM),
        scratch_shapes=[
            pltpu.VMEM((HEADS, 32, 256), BF),
            pltpu.VMEM((TP, 32, 256), BF),
            pltpu.VMEM((2, LAT, 256), BF),
            pltpu.VMEM((LAT, 512), BF),
            pltpu.VMEM((LAT, 512), BF),
            pltpu.VMEM((STEPS, 256, 256), BF),
            pltpu.VMEM((ROWS_DEV, LEN * ROPE), BF),
            pltpu.VMEM((STEPS, ROWS_DEV, LAT + ROPE), BF),
            pltpu.VMEM((ROWS_DEV, LEN, LAT), BF),
            pltpu.VMEM((YS, 256, COLS), BF),
            pltpu.VMEM((256, 256), BF),
            pltpu.VMEM((ROWS_DEV, LEN // 2, 128), BF),
            pltpu.VMEM((ROWS_DEV, LEN, 128), BF),
            pltpu.VMEM((STEPS, ROWS_DEV, 640), F32),
            pltpu.VMEM((STEPS, 2, 256, LAT), BF),
            pltpu.VMEM((STEPS, 2, TP, 16, LAT), BF),
            pltpu.VMEM((STEPS, TP, 16, 128), BF),
            pltpu.VMEM((ROWS_DEV, HEADS, LAT), BF),
            pltpu.VMEM((ROWS_DEV, HEADS, 128), BF),
            pltpu.VMEM((2, ROWS_DEV, 16, LAT), BF),
            pltpu.VMEM((STEPS, 2, TP, 16, LAT), BF),
            pltpu.VMEM((STEPS, 2, 256, LAT), BF),
            pltpu.VMEM((STEPS, 256, 256), BF),
            pltpu.VMEM((STEPS, YS, 256, 256), BF),
            pltpu.VMEM((CHUNKS, YS, ZS, 16, HALF), BF),
            pltpu.VMEM((CHUNKS, 2, YS, 16, HALF), BF),
            pltpu.VMEM(chunk, BF),
            pltpu.VMEM(chunk, BF),
            pltpu.VMEM(chunk, BF),
            dma((8,)),
            dma((15,)),
            dma((REPS,)),
            dma((TP,)),
            dma((TP,)),
            dma(()),
            dma(()),
            dma((YS,)),
            dma((YS,)),
            dma((YS,)),
            dma((YS,)),
            dma((TP,)),
            dma((TP,)),
            dma((STEPS, TP)),
            dma((STEPS, TP)),
            dma((STEPS, TP)),
            dma((STEPS, TP)),
            dma((STEPS, YS)),
            dma((STEPS, YS)),
            dma((CHUNKS, 2)),
            dma((CHUNKS, 2)),
            dma((CHUNKS,)),
            dma((CHUNKS,)),
            dma((CHUNKS, YS)),
            dma((CHUNKS, YS)),
        ],
        compiler_params=pltpu.CompilerParams(
            collective_id=0, has_side_effects=True, vmem_limit_bytes=56 * 2**20
        ),
        name="push_and_decode",
    )(
        bucket_slot,
        bucket_version,
        replica_version,
        old_scale,
        lengths,
        trainer_weight,
        old_weight,
        q_nope,
        q_rope,
        cache_latent,
        cache_rope,
        new_token,
        out_weight,
    )


def solution(mesh):
    return jax.shard_map(
        local,
        mesh=mesh,
        in_specs=(
            P("rep", "tp", None),
            P(),
            P(),
            P("rep", None),
            P("rep", None, "tp"),
            P("rep", None, "tp"),
            P(None, "rep", None, "tp"),
            P(None, "rep", None, "tp"),
            P("rep", "tp", None, None),
            P("rep", "tp", None),
            P(None, "rep", "tp", None),
            P("rep", "tp"),
            P("tp", None),
        ),
        out_specs=(P("rep", None, "tp"), P("rep", None, "tp"), P(None, "rep", "tp", None)),
        check_vma=False,
    )
```

```python
import jax
import jax.numpy as jnp
from jax import lax
from jax.experimental import pallas as pl
from jax.experimental.pallas import tpu as pltpu
from jax.sharding import PartitionSpec as P

HEADS = 32
LAT = 512
NOPE = 128
ROPE = 64
VDIM = 128
BLOCK = 128
STEPS = 2
PARTS = 2
D = 7168
LEN = 384
YS = 4
ZS = 4
TP = YS * ZS
REPS = 16
ROWS_DEV = 16
COLS = D // YS
HALF = COLS // 2
CHUNKS = 4
EPSILON = 1e-06
SCALING = (NOPE + ROPE) ** (-0.5)
MESH = pl.DeviceIdType.MESH
BF = jnp.bfloat16
F32 = jnp.float32
VM = pl.BlockSpec(memory_space=pltpu.VMEM)
SM = pl.BlockSpec(memory_space=pltpu.SMEM)
ANY = pl.BlockSpec(memory_space=pl.ANY)


def rem(a, b):
    return lax.rem(a, jnp.int32(b))


def div(a, b):
    return lax.div(a, jnp.int32(b))


def rcopy(src, dst, send_sem, recv_sem, **where):
    return pltpu.make_async_remote_copy(
        src_ref=src,
        dst_ref=dst,
        send_sem=send_sem,
        recv_sem=recv_sem,
        device_id=where,
        device_id_type=MESH,
    )


def greet(peers):
    barrier = pltpu.get_barrier_semaphore()
    for peer in peers:
        pl.semaphore_signal(barrier, inc=1, device_id=peer, device_id_type=MESH)
    pl.semaphore_wait(barrier, len(peers))


def mm(a, b, contract=((1,), (0,))):
    return lax.dot_general(a, b, (contract, ((), ())), preferred_element_type=F32)


def everything(
    slot_ref,
    bver_ref,
    rver_ref,
    oscale_ref,
    len_ref,
    tw_hbm,
    ow_hbm,
    qn_hbm,
    qp_hbm,
    cache_hbm,
    rope_hbm,
    tok_hbm,
    weight_hbm,
    sw_ref,
    ss_ref,
    dec,
    gath,
    sel,
    buck,
    ow,
    km,
    vm,
    qn,
    qn2,
    rope,
    tok,
    cache,
    wp,
    perm,
    ropes,
    kr,
    toks,
    qs,
    qr,
    qrr,
    qrow,
    qro,
    attr,
    ab,
    ar,
    ho,
    hg,
    pb,
    r1,
    fin,
    hl,
    lsem,
    gsend,
    grecv,
    tsend,
    trecv,
    csend,
    crecv,
    wsend,
    wrecv,
    xsend,
    xrecv,
    dsend,
    drecv,
    esend,
    erecv,
    vsend,
    vrecv,
    psend,
    precv,
    qsend,
    qrecv,
    asend,
    arecv,
    hsend,
    hrecv,
    s1send,
    s1recv,
    fsend,
    frecv,
):
    rep, tp = lax.axis_index("rep"), lax.axis_index("tp")
    zh, x, c = div(rep, 8), rem(div(rep, 2), 4), rem(rep, 2)
    y, z = div(tp, ZS), rem(tp, ZS)
    zpeer = rem(rep + 8, 16)
    cpeer = rep + 1 - 2 * c
    xpeers = [zh * 8 + rem(x + dx, 4) * 2 + c for dx in (1, 2, 3)]
    near = z + 1 - 2 * rem(z, 2)
    far = rem(z + 2, ZS)
    side, par = div(z, 2), rem(z, 2)
    mine = 2 * y + par
    share = 2 * x + c

    def rows16(t):
        return pl.ds(pl.multiple_of(16 * t, 16), 16)

    def rows32(t):
        return pl.ds(pl.multiple_of(32 * t, 32), 32)

    def columns(yy):
        return pl.ds(pl.multiple_of(COLS * yy, 256), COLS)

    def each(fn):
        def body(k, carry):
            fn(k)
            return carry

        lax.fori_loop(1, TP, body, 0)

    def source(k):
        return rem(tp + TP - k, TP)

    def slot_at(owner, reader_side):
        oz = rem(owner, ZS)
        return 8 * rem(div(oz, 2) + reader_side, 2) + 2 * div(owner, ZS) + rem(oz, 2)

    def kin(j):
        m = rem(mine + j, 8)
        return m, div(m, 2) * ZS + 2 * side + rem(m, 2)

    def each_kin(fn):
        def body(j, carry):
            fn(j)
            return carry

        lax.fori_loop(1, 8, body, 0)

    loads = [
        pltpu.make_async_copy(src, dst, lsem.at[i])
        for i, (src, dst) in enumerate(
            [
                (tw_hbm, gath.at[pl.ds(2 * rep, 2)]),
                (qp_hbm.at[:, 0, rows16(tp), :], qrr.at[:, mine]),
                (tok_hbm.at[:, 0], tok),
                (rope_hbm.at[0], rope),
                (ow_hbm.at[0], ow),
                (qn_hbm.at[:, 0], qn),
                (cache_hbm.at[0], cache),
                (weight_hbm.at[:, columns(y)], wp.at[y, pl.ds(0, 256), :]),
            ]
        )
    ]
    load_tw, load_qp, load_tok, load_rope, load_ow, load_qn, load_cache, load_w = loads
    for copy in loads:
        copy.start()
    greet(
        [{"tp": rem(tp + k, TP)} for k in range(1, TP)]
        + [{"rep": r} for r in [zpeer, cpeer] + xpeers]
        + [{"rep": zpeer, "tp": yy * ZS + far} for yy in range(YS)]
    )

    def block(b):
        return gath.at[pl.ds(2 * b, 2)]

    sent = []

    def pass_on(src, b, to):
        copy = rcopy(src, block(b), gsend.at[len(sent)], grecv.at[b], rep=to)
        copy.start()
        sent.append(copy)

    def arrived(b):
        rcopy(block(b), block(b), gsend.at[0], grecv.at[b], rep=zpeer).wait_recv()

    def part(src):
        return buck.at[c, rows32(src), :]

    def pick_copy(k):
        t = rem(tp + k, TP)
        return rcopy(sel.at[k], part(tp), tsend.at[k], trecv.at[tp], tp=t)

    def half(yy, core):
        return wp.at[yy, pl.ds(pl.multiple_of(128 * core, 128), 128), :]

    def shared(yy, who):
        return wp.at[yy, pl.ds(pl.multiple_of(256 + 32 * who, 32), 32), :]

    def all_shared(who):
        return wp.at[:, pl.ds(pl.multiple_of(256 + 32 * who, 32), 32), :]

    def far_weight_copy(yy):
        src = weight_hbm.at[pl.ds(pl.multiple_of(32 * share, 32), 32), columns(yy)]
        to = rem(rep + 8 * (1 - c), 16)
        return rcopy(src, shared(y, share), dsend.at[yy], drecv.at[y], rep=to, tp=yy * ZS + far)

    def spread_copy(dx):
        to = xpeers[dx - 1]
        return rcopy(all_shared(share), all_shared(share), esend.at[dx], erecv.at[x], rep=to)

    def spread_swap(dx):
        who = 2 * rem(x + dx, 4) + c
        return rcopy(all_shared(who), all_shared(who), esend.at[4 + dx], erecv.at[4 + rem(x + dx, 4)], rep=cpeer)

    def value_copy():
        return rcopy(vm.at[0], vm.at[1], vsend, vrecv, tp=y * ZS + far)

    def weight_copy(dy):
        to = rem(y + dy, YS)
        src = weight_hbm.at[pl.ds(pl.multiple_of(128 * c, 128), 128), columns(to)]
        return rcopy(src, half(y, c), wsend.at[dy], wrecv.at[y], tp=to * ZS + z)

    def swap_copy(dy):
        src = rem(y + YS - dy, YS)
        return rcopy(half(src, c), half(src, c), xsend.at[dy], xrecv.at[src], rep=cpeer)

    def rope_copy(k):
        t = rem(tp + k, TP)
        there = qrr.at[:, slot_at(tp, div(rem(t, ZS), 2))]
        return rcopy(qp_hbm.at[:, 0, rows16(t), :], there, psend.at[k], precv.at[tp], tp=t)

    def query_copy(p, k):
        t = rem(tp + k, TP)
        there = qr.at[p, :, slot_at(tp, div(rem(t, ZS), 2))]
        return rcopy(qs.at[p, :, rows16(t), :], there, qsend.at[p, k], qrecv.at[p, tp], tp=t)

    def back_copy(p, j):
        m, t = kin(j)
        there = ar.at[p, :, :, rows16(mine), :]
        return rcopy(ab.at[p, :, :, m], there, asend.at[p, j], arecv.at[p, mine], tp=t)

    def gather_copy(p, dy):
        to = rem(y + dy, YS) * ZS + z
        return rcopy(ho.at[p], hg.at[p, y], hsend.at[p, dy], hrecv.at[p, y], tp=to)

    def near_copy(q):
        return rcopy(pb.at[q, :, 1 - par], r1.at[q], s1send.at[q], s1recv.at[q], tp=y * ZS + near)

    def home_copy(q, dy):
        to = rem(y + dy, YS)
        return rcopy(fin.at[q, to], hl.at[q, y], fsend.at[q, dy], frecv.at[q, y], tp=to * ZS + z)

    for to in [zpeer] + xpeers + [cpeer]:
        pass_on(tw_hbm, rep, to)
    weight_copy(1).start()
    weight_copy(3).start()
    arrived(zpeer)
    for to in xpeers + [cpeer]:
        pass_on(block(zpeer), zpeer, to)
    for yy in range(YS):
        far_weight_copy(yy).start()
    for xp in xpeers:
        arrived(xp)
        pass_on(block(xp), xp, cpeer)
    for xp in xpeers:
        b = rem(xp + 8, 16)
        arrived(b)
        pass_on(block(b), b, cpeer)
    load_tw.wait()
    for b in [cpeer, rem(cpeer + 8, 16)]:
        arrived(b)
    for xp in xpeers:
        other = xp + 1 - 2 * c
        arrived(other)
        arrived(rem(other + 8, 16))

    def pick(k):
        sel[k] = gath[slot_ref[2 * rem(tp + k, TP) + c]]
        pick_copy(k).start()

    each(pick)
    buck[c, rows32(tp), :] = gath[slot_ref[2 * tp + c]]
    each(lambda k: rope_copy(k).start())
    weight_copy(2).start()

    pi = lax.broadcasted_iota(jnp.int32, (256, 256), 0)
    pj = lax.broadcasted_iota(jnp.int32, (256, 256), 1)
    swapped = ((pi >> 4) == (pj & 15)) & ((pi & 15) == (pj >> 4))
    perm[...] = jnp.where(swapped, 1.0, 0.0).astype(BF)
    load_tok.wait()
    toks[...] = jnp.zeros_like(toks)
    toks[:, :, 0 : LAT + ROPE] = tok[...].astype(F32)
    load_rope.wait()
    for g in range(12):
        tiles = [rope[:, (16 * g + i) * 128 : (16 * g + i + 1) * 128] for i in range(16)]
        turned = mm(perm[...], jnp.concatenate(tiles, axis=0)).astype(BF)
        ropes[:, 16 * g : 16 * (g + 1), :] = turned.reshape(16, 16, 128)

    load_qn.wait()

    def reorder(t, carry):
        first = qn[0, rows16(t), :].astype(F32)
        second = qn[1, rows16(t), :].astype(F32)
        for p in range(PARTS):
            rows = slice(8 * p, 8 * p + 8)
            both = jnp.concatenate([first[rows], second[rows]], axis=0)
            qn2[p, rows16(t), :] = both.astype(BF)
        return carry

    lax.fori_loop(0, TP, reorder, 0)

    def bucket_arrived(k):
        src = source(k)
        rcopy(part(src), part(src), tsend.at[k], trecv.at[src], tp=src).wait_recv()

    each(bucket_arrived)
    swap = rcopy(buck.at[c], buck.at[c], csend, crecv, rep=cpeer)
    swap.start()
    load_ow.wait()
    rcopy(buck.at[1 - c], buck.at[1 - c], csend, crecv, rep=cpeer).wait_recv()

    cell_row = lax.broadcasted_iota(jnp.int32, (4, 4), 0)
    cell_col = lax.broadcasted_iota(jnp.int32, (4, 4), 1)

    def serve(hh, cc, scales):
        head = 2 * tp + hh
        stale = (rver_ref[0, head] != bver_ref[head]).astype(jnp.int32)
        col = hh * 256 + cc * BLOCK
        for i in range(4):
            rows = slice(i * BLOCK, (i + 1) * BLOCK)
            raw = buck[hh, rows, cc * BLOCK : (cc + 1) * BLOCK].astype(F32)
            peak = jnp.max(jnp.abs(raw), axis=0, keepdims=True)
            peak = jnp.max(peak, axis=1, keepdims=True)
            scale = peak + EPSILON
            fresh = (raw / scale).astype(BF).astype(F32)
            old = ow[rows, col : col + BLOCK].astype(F32)
            served = jnp.where(jnp.zeros((BLOCK, BLOCK), jnp.int32) + stale != 0, fresh, old)
            held = jnp.zeros((1, 1), F32) + oscale_ref[0, i, 2 * hh + cc]
            used = jnp.where(jnp.zeros((1, 1), jnp.int32) + stale != 0, scale, held)
            sw_ref[0, rows, col : col + BLOCK] = served.astype(BF)
            maps = km if cc == 0 else vm.at[0]
            maps[rows, hh * BLOCK : (hh + 1) * BLOCK] = (served * used).astype(BF)
            here = (cell_row == i) & (cell_col == 2 * hh + cc)
            scales = jnp.where(here, used, scales)
        return scales

    scales = jnp.zeros((4, 4), F32)
    for hh in range(2):
        scales = serve(hh, 0, scales)

    for p in range(PARTS):
        for hh in range(2):
            qs[p, hh] = mm(
                qn2[p, :, hh * NOPE : (hh + 1) * NOPE],
                km[:, hh * BLOCK : (hh + 1) * BLOCK],
                ((1,), (1,)),
            ).astype(BF)
        each(lambda k: query_copy(p, k).start())
    for hh in range(2):
        scales = serve(hh, 1, scales)
    ss_ref[0] = scales
    for p in range(PARTS):
        for hh in range(2):
            qr[p, hh, mine] = qs[p, hh, rows16(tp), :]
    for yy in range(YS):
        there = shared(yy, share)
        rcopy(there, there, dsend.at[yy], drecv.at[yy], tp=yy * ZS + far).wait_recv()
    for dx in (1, 2, 3):
        spread_copy(dx).start()
    spread_swap(0).start()

    si = lax.broadcasted_iota(jnp.int32, (LEN, LEN // 2), 0)
    sj = lax.broadcasted_iota(jnp.int32, (LEN, LEN // 2), 1)
    spread = jnp.where((si >> 1) == sj, 1.0, 0.0).astype(BF)
    ki = lax.broadcasted_iota(jnp.int32, (LEN, 128), 0)
    kj = lax.broadcasted_iota(jnp.int32, (LEN, 128), 1)
    kept = (ki & 1) == (kj >> 6)

    def place(r, carry):
        kr[r] = jnp.where(kept, mm(spread, ropes[r]), 0.0).astype(BF)
        return carry

    lax.fori_loop(0, ROWS_DEV, place, 0)
    load_cache.wait()
    load_qp.wait()

    di = lax.broadcasted_iota(jnp.int32, (128, 256), 0)
    dj = lax.broadcasted_iota(jnp.int32, (128, 256), 1)
    double = jnp.where(di == (dj >> 7) * 64 + (dj & 63), 1.0, 0.0).astype(BF)
    position = lax.broadcasted_iota(jnp.int32, (1, LEN), 1)

    def rope_arrived(k):
        src = source(k)
        there = qrr.at[:, slot_at(src, side)]
        rcopy(there, there, psend.at[k], precv.at[src], tp=src).wait_recv()

    each(rope_arrived)
    for s in range(STEPS):
        turned = mm(perm[...], qrr[s].reshape(256, 128)).astype(BF)
        turned = mm(turned, double).astype(BF)
        for hh in range(2):
            first = 16 * (2 * s + hh)
            qro[:, first : first + 16, :] = turned[:, 128 * hh : 128 * (hh + 1)].reshape(16, 16, 128)
    late = lax.broadcasted_iota(jnp.int32, (2 * HEADS, 1), 0) >= HEADS

    def weights_arrived():
        for dy in (1, 2, 3):
            src = rem(y + YS - dy, YS)
            there = half(src, c)
            rcopy(there, there, wsend.at[dy], wrecv.at[src], tp=src * ZS + z).wait_recv()
            swap_copy(dy).start()

    def spread_arrived():
        for dx in (1, 2, 3):
            xx = rem(x + dx, 4)
            there = all_shared(2 * xx + c)
            rcopy(there, there, esend.at[dx], erecv.at[xx], rep=cpeer).wait_recv()
            spread_swap(dx).start()

    def attend(p):
        def query_arrived(k):
            src = source(k)
            there = qr.at[p, :, slot_at(src, side)]
            rcopy(there, there, qsend.at[p, k], qrecv.at[p, src], tp=src).wait_recv()

        each(query_arrived)
        for hh in range(2):
            turned = mm(perm[...], qr[p, hh].reshape(256, LAT)).astype(BF)
            turned = turned.reshape(2, 8, 16, LAT)
            for s in range(STEPS):
                first = 16 * (2 * s + hh)
                qrow[:, first : first + 16, :] = turned[s]

        def attend_row(i, carry):
            r = 8 * p + i
            q_lat, q_rope, keys = qrow[i], qro[r], cache[r]
            score = mm(q_lat, keys, ((1,), (1,))) + mm(q_rope, kr[r], ((1,), (1,)))
            score = jnp.where(position < len_ref[0, r], score * SCALING, -jnp.inf)
            top = jnp.max(score, axis=1, keepdims=True)
            lat32, rope32 = q_lat.astype(F32), q_rope.astype(F32)
            news = []
            for t in range(STEPS):
                tok_r = toks[t, pl.ds(r, 1), :]
                new = jnp.sum(lat32 * tok_r[:, :LAT], axis=1, keepdims=True)
                new = new + jnp.sum(rope32 * tok_r[:, LAT:], axis=1, keepdims=True)
                new = new * SCALING
                if t == 1:
                    new = jnp.where(late, new, -jnp.inf)
                news.append((new, tok_r[:, :LAT]))
            for new, _ in news:
                top = jnp.maximum(top, new)
            expped = jnp.exp(score - top)
            new_exp = [jnp.exp(new - top) for new, _ in news]
            total = jnp.sum(expped, axis=1, keepdims=True)
            for e in new_exp:
                total = total + e
            inverse = 1.0 / total
            out = mm((expped * inverse).astype(BF), keys)
            for e, (_, tok_r) in zip(new_exp, news):
                out = out + (e * inverse).astype(BF).astype(F32) * tok_r
            out = out.astype(BF)
            for s in range(STEPS):
                for hh in range(2):
                    first = 16 * (2 * s + hh)
                    attr[hh, 8 * s + i] = out[first : first + 16]
            return carry

        lax.fori_loop(0, 8, attend_row, 0, unroll=4)
        for hh in range(2):
            turned = mm(perm[...], attr[hh].reshape(256, LAT)).astype(BF)
            ab[p, hh] = turned.reshape(2, 8, 16, LAT)
        each_kin(lambda j: back_copy(p, j).start())
        for hh in range(2):
            for f in range(2):
                ar[p, hh, f, rows16(mine), :] = ab[p, hh, f, mine]

    def heads_out(p):
        def back_arrived(j):
            m, t = kin(8 - j)
            there = ar.at[p, :, :, rows16(m), :]
            rcopy(there, there, asend.at[p, j], arecv.at[p, m], tp=t).wait_recv()

        each_kin(back_arrived)
        for f in range(2):
            for hh in range(2):
                first = 256 * f + VDIM * hh
                ho[p, :, first : first + VDIM] = mm(
                    ar[p, hh, f], vm[f, :, hh * VDIM : (hh + 1) * VDIM]
                ).astype(BF)
        for dy in (1, 2, 3):
            gather_copy(p, dy).start()
        hg[p, y] = ho[p]

    def multiply(p):
        for dy in (1, 2, 3):
            src = rem(y + YS - dy, YS)
            there = hg.at[p, src]
            rcopy(there, there, hsend.at[p, dy], hrecv.at[p, src], tp=src * ZS + z).wait_recv()
        for q in (2 * p, 2 * p + 1):
            for first, width in ((0, 512), (512, 384)):
                cols = slice(HALF * (q % 2) + first, HALF * (q % 2) + first + width)
                total = mm(hg[p, 0], wp[0, :, cols])
                for k in range(1, YS):
                    total = total + mm(hg[p, k], wp[k, :, cols])
                pb[q, :, :, :, first : first + width] = total.astype(BF).reshape(YS, 2, 16, width)
            near_copy(q).start()

    def finish(q):
        near_copy(q).wait_recv()
        fin[q] = (pb[q, :, par].astype(F32) + r1[q].astype(F32)).astype(BF)
        for dy in (1, 2, 3):
            home_copy(q, dy).start()
        hl[q, y] = fin[q, y]

    attend(0)
    value_copy().start()
    weights_arrived()
    attend(1)
    spread_arrived()
    value_copy().wait_recv()
    heads_out(0)
    load_w.wait()
    for dy in (1, 2, 3):
        src = rem(y + YS - dy, YS)
        there = half(src, 1 - c)
        rcopy(there, there, xsend.at[dy], xrecv.at[src], rep=cpeer).wait_recv()
    for xx in range(4):
        there = all_shared(2 * xx + 1 - c)
        rcopy(there, there, esend.at[4], erecv.at[4 + xx], rep=cpeer).wait_recv()
    multiply(0)
    heads_out(1)
    finish(0)
    multiply(1)
    finish(1)
    finish(2)
    finish(3)

    for q in range(CHUNKS):
        for dy in (1, 2, 3):
            src = rem(y + YS - dy, YS)
            there = hl.at[q, src]
            rcopy(there, there, fsend.at[q, dy], frecv.at[q, src], tp=src * ZS + z).wait_recv()
    for side_cols in range(2):
        for yy in range(YS):
            first = COLS * yy + HALF * side_cols
            top = hl[side_cols, yy].astype(F32)
            low = hl[2 + side_cols, yy].astype(F32)
            for s in range(STEPS):
                rows = slice(8 * s, 8 * s + 8)
                both = jnp.concatenate([top[rows], low[rows]], axis=0)
                dec[s, 0, :, first : first + HALF] = both.astype(BF)

    for copy in sent:
        copy.wait_send()
    each(lambda k: pick_copy(k).wait_send())
    swap.wait_send()
    each(lambda k: rope_copy(k).wait_send())
    for dy in (1, 2, 3):
        weight_copy(dy).wait_send()
        swap_copy(dy).wait_send()
    for yy in range(YS):
        far_weight_copy(yy).wait_send()
    for dx in range(4):
        if dx > 0:
            spread_copy(dx).wait_send()
        spread_swap(dx).wait_send()
    value_copy().wait_send()
    for p in range(PARTS):
        each(lambda k: query_copy(p, k).wait_send())
        each_kin(lambda j: back_copy(p, j).wait_send())
        for dy in (1, 2, 3):
            gather_copy(p, dy).wait_send()
    for q in range(CHUNKS):
        near_copy(q).wait_send()
        for dy in (1, 2, 3):
            home_copy(q, dy).wait_send()


def local(
    trainer_weight,
    bucket_slot,
    bucket_version,
    replica_version,
    old_weight,
    old_scale,
    q_nope,
    q_rope,
    cache_latent,
    cache_rope,
    new_token,
    lengths,
    out_weight,
):
    dma = pltpu.SemaphoreType.DMA
    chunk = (CHUNKS, YS, 16, HALF)
    return pl.pallas_call(
        everything,
        out_shape=(
            jax.ShapeDtypeStruct((1, LAT, 512), BF),
            jax.ShapeDtypeStruct((1, 4, 4), F32),
            jax.ShapeDtypeStruct((STEPS, 1, 16, D), BF),
        ),
        in_specs=[SM] * 5 + [ANY] * 8,
        out_specs=(VM, VM, VM),
        scratch_shapes=[
            pltpu.VMEM((HEADS, 32, 256), BF),
            pltpu.VMEM((TP, 32, 256), BF),
            pltpu.VMEM((2, LAT, 256), BF),
            pltpu.VMEM((LAT, 512), BF),
            pltpu.VMEM((LAT, 256), BF),
            pltpu.VMEM((2, LAT, 256), BF),
            pltpu.VMEM((STEPS, 256, 256), BF),
            pltpu.VMEM((PARTS, 256, 256), BF),
            pltpu.VMEM((ROWS_DEV, LEN * ROPE), BF),
            pltpu.VMEM((STEPS, ROWS_DEV, LAT + ROPE), BF),
            pltpu.VMEM((ROWS_DEV, LEN, LAT), BF),
            pltpu.VMEM((YS, 512, COLS), BF),
            pltpu.VMEM((256, 256), BF),
            pltpu.VMEM((ROWS_DEV, LEN // 2, 128), BF),
            pltpu.VMEM((ROWS_DEV, LEN, 128), BF),
            pltpu.VMEM((STEPS, ROWS_DEV, 640), F32),
            pltpu.VMEM((PARTS, 2, 256, LAT), BF),
            pltpu.VMEM((PARTS, 2, TP, 16, LAT), BF),
            pltpu.VMEM((STEPS, TP, 16, 128), BF),
            pltpu.VMEM((8, 2 * HEADS, LAT), BF),
            pltpu.VMEM((ROWS_DEV, 2 * HEADS, 128), BF),
            pltpu.VMEM((2, 16, 16, LAT), BF),
            pltpu.VMEM((PARTS, 2, 2, 8, 16, LAT), BF),
            pltpu.VMEM((PARTS, 2, 2, 128, LAT), BF),
            pltpu.VMEM((PARTS, 128, 512), BF),
            pltpu.VMEM((PARTS, YS, 128, 512), BF),
            pltpu.VMEM((CHUNKS, YS, 2, 16, HALF), BF),
            pltpu.VMEM(chunk, BF),
            pltpu.VMEM(chunk, BF),
            pltpu.VMEM(chunk, BF),
            dma((8,)),
            dma((15,)),
            dma((REPS,)),
            dma((TP,)),
            dma((TP,)),
            dma(()),
            dma(()),
            dma((YS,)),
            dma((YS,)),
            dma((YS,)),
            dma((YS,)),
            dma((YS,)),
            dma((YS,)),
            dma((8,)),
            dma((8,)),
            dma(()),
            dma(()),
            dma((TP,)),
            dma((TP,)),
            dma((PARTS, TP)),
            dma((PARTS, TP)),
            dma((PARTS, 8)),
            dma((PARTS, 8)),
            dma((PARTS, YS)),
            dma((PARTS, YS)),
            dma((CHUNKS,)),
            dma((CHUNKS,)),
            dma((CHUNKS, YS)),
            dma((CHUNKS, YS)),
        ],
        compiler_params=pltpu.CompilerParams(
            collective_id=0, has_side_effects=True, vmem_limit_bytes=56 * 2**20
        ),
        name="push_and_decode",
    )(
        bucket_slot,
        bucket_version,
        replica_version,
        old_scale,
        lengths,
        trainer_weight,
        old_weight,
        q_nope,
        q_rope,
        cache_latent,
        cache_rope,
        new_token,
        out_weight,
    )


def solution(mesh):
    return jax.shard_map(
        local,
        mesh=mesh,
        in_specs=(
            P("rep", "tp", None),
            P(),
            P(),
            P("rep", None),
            P("rep", None, "tp"),
            P("rep", None, "tp"),
            P(None, "rep", None, "tp"),
            P(None, "rep", None, "tp"),
            P("rep", "tp", None, None),
            P("rep", "tp", None),
            P(None, "rep", "tp", None),
            P("rep", "tp"),
            P("tp", None),
        ),
        out_specs=(P("rep", None, "tp"), P("rep", None, "tp"), P(None, "rep", "tp", None)),
        check_vma=False,
    )
```

```python
import jax
import jax.numpy as jnp
from jax import lax
from jax.experimental import pallas as pl
from jax.experimental.pallas import tpu as pltpu
from jax.sharding import PartitionSpec as P

HEADS = 32
LAT = 512
NOPE = 128
ROPE = 64
VDIM = 128
BLOCK = 128
STEPS = 2
PARTS = 2
D = 7168
LEN = 384
YS = 4
ZS = 4
TP = YS * ZS
REPS = 16
ROWS_DEV = 16
COLS = D // YS
HALF = COLS // 2
CHUNKS = 4
EPSILON = 1e-06
SCALING = (NOPE + ROPE) ** (-0.5)
MESH = pl.DeviceIdType.MESH
BF = jnp.bfloat16
F32 = jnp.float32
VM = pl.BlockSpec(memory_space=pltpu.VMEM)
SM = pl.BlockSpec(memory_space=pltpu.SMEM)
HB = pl.BlockSpec(memory_space=pltpu.HBM)


def rem(a, b):
    return lax.rem(a, jnp.int32(b))


def div(a, b):
    return lax.div(a, jnp.int32(b))


def rcopy(src, dst, send_sem, recv_sem, **where):
    return pltpu.make_async_remote_copy(
        src_ref=src,
        dst_ref=dst,
        send_sem=send_sem,
        recv_sem=recv_sem,
        device_id=where,
        device_id_type=MESH,
    )


def greet(peers):
    barrier = pltpu.get_barrier_semaphore()
    for peer in peers:
        pl.semaphore_signal(barrier, inc=1, device_id=peer, device_id_type=MESH)
    pl.semaphore_wait(barrier, len(peers))


def mm(a, b, contract=((1,), (0,))):
    return lax.dot_general(a, b, (contract, ((), ())), preferred_element_type=F32)


def everything(
    slot_ref,
    bver_ref,
    rver_ref,
    oscale_ref,
    len_ref,
    tw_hbm,
    ow_hbm,
    qn_hbm,
    qp_hbm,
    cache_hbm,
    rope_hbm,
    tok_hbm,
    weight_hbm,
    sw_ref,
    ss_ref,
    dec,
    gath,
    sel,
    buck,
    ow,
    km,
    vm,
    qn,
    qn2,
    rope,
    tok,
    cache,
    wp,
    perm,
    ropes,
    kr,
    toks,
    qs,
    qr,
    qrr,
    qrow,
    qro,
    attr,
    ab,
    ar,
    ho,
    hg,
    pb,
    hl,
    lsem,
    gsend,
    grecv,
    tsend,
    trecv,
    csend,
    crecv,
    wsend,
    wrecv,
    xsend,
    xrecv,
    dsend,
    drecv,
    vsend,
    vrecv,
    psend,
    precv,
    qsend,
    qrecv,
    asend,
    arecv,
    hsend,
    hrecv,
    fsend,
    frecv,
):
    rep, tp = lax.axis_index("rep"), lax.axis_index("tp")
    zh, x, c = div(rep, 8), rem(div(rep, 2), 4), rem(rep, 2)
    y, z = div(tp, ZS), rem(tp, ZS)
    zpeer = rem(rep + 8, 16)
    cpeer = rep + 1 - 2 * c
    xpeers = [zh * 8 + rem(x + dx, 4) * 2 + c for dx in (1, 2, 3)]
    far = rem(z + 2, ZS)
    side, par = div(z, 2), rem(z, 2)
    mine = 2 * y + par
    share = 2 * x + c

    def rows16(t):
        return pl.ds(pl.multiple_of(16 * t, 16), 16)

    def rows32(t):
        return pl.ds(pl.multiple_of(32 * t, 32), 32)

    def columns(yy):
        return pl.ds(pl.multiple_of(COLS * yy, 256), COLS)

    def each(fn):
        def body(k, carry):
            fn(k)
            return carry

        lax.fori_loop(1, TP, body, 0)

    def source(k):
        return rem(tp + TP - k, TP)

    def slot_at(owner, reader_side):
        oz = rem(owner, ZS)
        return 8 * rem(div(oz, 2) + reader_side, 2) + 2 * div(owner, ZS) + rem(oz, 2)

    def kin(j):
        m = rem(mine + j, 8)
        return m, div(m, 2) * ZS + 2 * side + rem(m, 2)

    def each_kin(fn):
        def body(j, carry):
            fn(j)
            return carry

        lax.fori_loop(1, 8, body, 0)

    loads = [
        pltpu.make_async_copy(src, dst, lsem.at[i])
        for i, (src, dst) in enumerate(
            [
                (tw_hbm, gath.at[pl.ds(2 * rep, 2)]),
                (qp_hbm.at[:, 0, rows16(tp), :], qrr.at[:, mine]),
                (tok_hbm.at[:, 0], tok),
                (rope_hbm.at[0], rope),
                (ow_hbm.at[0], ow),
                (qn_hbm.at[:, 0], qn),
                (cache_hbm.at[0], cache),
                (weight_hbm.at[:, columns(y)], wp.at[0, pl.ds(0, 256), :]),
            ]
        )
    ]
    load_tw, load_qp, load_tok, load_rope, load_ow, load_qn, load_cache, load_w = loads
    for copy in loads:
        copy.start()
    greet(
        [{"tp": rem(tp + k, TP)} for k in range(1, TP)]
        + [{"rep": r} for r in xpeers + [zpeer, cpeer]]
        + [{"rep": zpeer, "tp": yy * ZS + far} for yy in range(YS)]
    )

    def block(b):
        return gath.at[pl.ds(2 * b, 2)]

    sent = []

    def pass_on(src, b, to):
        copy = rcopy(src, block(b), gsend.at[len(sent)], grecv.at[b], rep=to)
        copy.start()
        sent.append(copy)

    def arrived(b):
        rcopy(block(b), block(b), gsend.at[0], grecv.at[b], rep=zpeer).wait_recv()

    def part(src):
        return buck.at[c, rows32(src), :]

    def pick_copy(k):
        t = rem(tp + k, TP)
        return rcopy(sel.at[k], part(tp), tsend.at[k], trecv.at[tp], tp=t)

    def swap_bucket():
        return rcopy(buck.at[c], buck.at[c], csend, crecv, rep=cpeer)

    def eighth(f, who):
        return pl.ds(pl.multiple_of(256 * f + 32 * who, 32), 32)

    def eighths(f, who):
        return wp.at[pl.ds(1 - f, 3 + f), eighth(f, who), :]

    own_eighth = pl.ds(pl.multiple_of(32 * share, 32), 32)

    def weight_copy(f, dy):
        yy = rem(y + dy, YS)
        src = weight_hbm.at[own_eighth, columns(yy)]
        there = wp.at[(YS - dy) % YS, eighth(f, share), :]
        if f == 0:
            return rcopy(src, there, wsend.at[f, dy], wrecv.at[f, (YS - dy) % YS], tp=yy * ZS + z)
        to = rem(rep + 8 * (1 - c), 16)
        return rcopy(src, there, wsend.at[f, dy], wrecv.at[f, (YS - dy) % YS], rep=to, tp=yy * ZS + far)

    def spread_copy(f, dx):
        here = eighths(f, share)
        return rcopy(here, here, xsend.at[f, dx], xrecv.at[f, x], rep=xpeers[dx - 1])

    def core_copy(f, dx):
        xx = rem(x + dx, 4)
        here = eighths(f, 2 * xx + c)
        return rcopy(here, here, dsend.at[f, dx], drecv.at[f, xx], rep=cpeer)

    def spread_weights(f):
        for j in range(1 - f, YS):
            there = wp.at[j, eighth(f, share), :]
            rcopy(there, there, wsend.at[f, j], wrecv.at[f, j], rep=cpeer).wait_recv()
        for dx in (2, 1, 3):
            spread_copy(f, dx).start()
        core_copy(f, 0).start()

    def share_weights(f):
        for dx in (1, 3, 2):
            xx = rem(x + dx, 4)
            there = eighths(f, 2 * xx + c)
            rcopy(there, there, xsend.at[f, dx], xrecv.at[f, xx], rep=cpeer).wait_recv()
            core_copy(f, dx).start()

    def weights_arrived(f):
        for xx in range(4):
            there = eighths(f, 2 * xx + 1 - c)
            rcopy(there, there, dsend.at[f, 0], drecv.at[f, xx], rep=cpeer).wait_recv()

    def value_copy():
        return rcopy(vm.at[0], vm.at[1], vsend, vrecv, tp=y * ZS + far)

    def rope_copy(k):
        t = rem(tp + k, TP)
        there = qrr.at[:, slot_at(tp, div(rem(t, ZS), 2))]
        return rcopy(qp_hbm.at[:, 0, rows16(t), :], there, psend.at[k], precv.at[tp], tp=t)

    def query_copy(p, k):
        t = rem(tp + k, TP)
        there = qr.at[p, :, slot_at(tp, div(rem(t, ZS), 2))]
        return rcopy(qs.at[p, :, rows16(t), :], there, qsend.at[p, k], qrecv.at[p, tp], tp=t)

    def back_copy(p, j):
        m, t = kin(j)
        there = ar.at[p, :, :, rows16(mine), :]
        return rcopy(ab.at[p, :, :, m], there, asend.at[p, j], arecv.at[p, mine], tp=t)

    def gather_copy(p, dy):
        to = rem(y + dy, YS) * ZS + z
        return rcopy(ho.at[p], hg.at[p, YS - dy], hsend.at[p, dy], hrecv.at[p, YS - dy], tp=to)

    def home_copy(q, j):
        m, t = kin(j)
        there = hl.at[q, y, par]
        return rcopy(pb.at[q, div(m, 2), rem(m, 2)], there, fsend.at[q, j], frecv.at[q, mine], tp=t)

    for to in [zpeer] + xpeers + [cpeer]:
        pass_on(tw_hbm, rep, to)
    for dy in (2, 1, 3):
        weight_copy(0, dy).start()
    arrived(zpeer)
    for to in xpeers + [cpeer]:
        pass_on(block(zpeer), zpeer, to)
    for dy in range(YS):
        weight_copy(1, dy).start()
    for xp in xpeers:
        arrived(xp)
        pass_on(block(xp), xp, cpeer)
    for xp in xpeers:
        b = rem(xp + 8, 16)
        arrived(b)
        pass_on(block(b), b, cpeer)
    load_tw.wait()
    for b in [zpeer, rep] + xpeers + [rem(xp + 8, 16) for xp in xpeers]:
        arrived(b + 1 - 2 * c)

    def pick(k):
        sel[k] = gath[slot_ref[2 * rem(tp + k, TP) + c]]
        pick_copy(k).start()

    each(pick)
    buck[c, rows32(tp), :] = gath[slot_ref[2 * tp + c]]
    spread_weights(0)
    each(lambda k: rope_copy(k).start())

    pi = lax.broadcasted_iota(jnp.int32, (256, 256), 0)
    pj = lax.broadcasted_iota(jnp.int32, (256, 256), 1)
    swapped = ((pi >> 4) == (pj & 15)) & ((pi & 15) == (pj >> 4))
    perm[...] = jnp.where(swapped, 1.0, 0.0).astype(BF)
    load_tok.wait()
    toks[...] = jnp.zeros_like(toks)
    toks[:, :, 0 : LAT + ROPE] = tok[...].astype(F32)
    load_rope.wait()
    for g in range(12):
        tiles = [rope[:, (16 * g + i) * 128 : (16 * g + i + 1) * 128] for i in range(16)]
        turned = mm(perm[...], jnp.concatenate(tiles, axis=0)).astype(BF)
        ropes[:, 16 * g : 16 * (g + 1), :] = turned.reshape(16, 16, 128)

    load_qn.wait()

    def reorder(t, carry):
        first = qn[0, rows16(t), :].astype(F32)
        second = qn[1, rows16(t), :].astype(F32)
        for p in range(PARTS):
            rows = slice(8 * p, 8 * p + 8)
            both = jnp.concatenate([first[rows], second[rows]], axis=0)
            qn2[p, rows16(t), :] = both.astype(BF)
        return carry

    lax.fori_loop(0, TP, reorder, 0)

    load_ow.wait()

    def bucket_arrived(k):
        src = source(k)
        rcopy(part(src), part(src), tsend.at[k], trecv.at[src], tp=src).wait_recv()

    each(bucket_arrived)
    swap_bucket().start()
    there = buck.at[1 - c]
    rcopy(there, there, csend, crecv, rep=cpeer).wait_recv()

    cell_row = lax.broadcasted_iota(jnp.int32, (4, 4), 0)
    cell_col = lax.broadcasted_iota(jnp.int32, (4, 4), 1)

    def serve(hh, cc, scales):
        head = 2 * tp + hh
        stale = (rver_ref[0, head] != bver_ref[head]).astype(jnp.int32)
        col = hh * 256 + cc * BLOCK
        for i in range(4):
            rows = slice(i * BLOCK, (i + 1) * BLOCK)
            raw = buck[hh, rows, cc * BLOCK : (cc + 1) * BLOCK].astype(F32)
            peak = jnp.max(jnp.abs(raw), axis=0, keepdims=True)
            peak = jnp.max(peak, axis=1, keepdims=True)
            scale = peak + EPSILON
            fresh = (raw / scale).astype(BF).astype(F32)
            old = ow[rows, col : col + BLOCK].astype(F32)
            served = jnp.where(jnp.zeros((BLOCK, BLOCK), jnp.int32) + stale != 0, fresh, old)
            held = jnp.zeros((1, 1), F32) + oscale_ref[0, i, 2 * hh + cc]
            used = jnp.where(jnp.zeros((1, 1), jnp.int32) + stale != 0, scale, held)
            sw_ref[0, rows, col : col + BLOCK] = served.astype(BF)
            maps = km if cc == 0 else vm.at[0]
            maps[rows, hh * BLOCK : (hh + 1) * BLOCK] = (served * used).astype(BF)
            here = (cell_row == i) & (cell_col == 2 * hh + cc)
            scales = jnp.where(here, used, scales)
        return scales

    scales = jnp.zeros((4, 4), F32)
    for hh in range(2):
        scales = serve(hh, 0, scales)

    for p in range(PARTS):
        for hh in range(2):
            qs[p, hh] = mm(
                qn2[p, :, hh * NOPE : (hh + 1) * NOPE],
                km[:, hh * BLOCK : (hh + 1) * BLOCK],
                ((1,), (1,)),
            ).astype(BF)
        each(lambda k: query_copy(p, k).start())
    spread_weights(1)
    for hh in range(2):
        scales = serve(hh, 1, scales)
    ss_ref[0] = scales
    for p in range(PARTS):
        for hh in range(2):
            qr[p, hh, mine] = qs[p, hh, rows16(tp), :]

    si = lax.broadcasted_iota(jnp.int32, (LEN, LEN // 2), 0)
    sj = lax.broadcasted_iota(jnp.int32, (LEN, LEN // 2), 1)
    spread = jnp.where((si >> 1) == sj, 1.0, 0.0).astype(BF)
    ki = lax.broadcasted_iota(jnp.int32, (LEN, 128), 0)
    kj = lax.broadcasted_iota(jnp.int32, (LEN, 128), 1)
    kept = (ki & 1) == (kj >> 6)

    def place(r, carry):
        kr[r] = jnp.where(kept, mm(spread, ropes[r]), 0.0).astype(BF)
        return carry

    lax.fori_loop(0, ROWS_DEV, place, 0)
    load_cache.wait()
    load_qp.wait()

    di = lax.broadcasted_iota(jnp.int32, (128, 256), 0)
    dj = lax.broadcasted_iota(jnp.int32, (128, 256), 1)
    double = jnp.where(di == (dj >> 7) * 64 + (dj & 63), 1.0, 0.0).astype(BF)
    position = lax.broadcasted_iota(jnp.int32, (1, LEN), 1)

    def rope_arrived(k):
        src = source(k)
        there = qrr.at[:, slot_at(src, side)]
        rcopy(there, there, psend.at[k], precv.at[src], tp=src).wait_recv()

    each(rope_arrived)
    for s in range(STEPS):
        turned = mm(perm[...], qrr[s].reshape(256, 128)).astype(BF)
        turned = mm(turned, double).astype(BF)
        for hh in range(2):
            first = 16 * (2 * s + hh)
            qro[:, first : first + 16, :] = turned[:, 128 * hh : 128 * (hh + 1)].reshape(16, 16, 128)
    late = lax.broadcasted_iota(jnp.int32, (2 * HEADS, 1), 0) >= HEADS

    def attend(p):
        def query_arrived(k):
            src = source(k)
            there = qr.at[p, :, slot_at(src, side)]
            rcopy(there, there, qsend.at[p, k], qrecv.at[p, src], tp=src).wait_recv()

        each(query_arrived)
        for hh in range(2):
            turned = mm(perm[...], qr[p, hh].reshape(256, LAT)).astype(BF)
            turned = turned.reshape(2, 8, 16, LAT)
            for s in range(STEPS):
                first = 16 * (2 * s + hh)
                qrow[:, first : first + 16, :] = turned[s]

        def attend_row(i, carry):
            r = 8 * p + i
            q_lat, q_rope, keys = qrow[i], qro[r], cache[r]
            score = mm(q_lat, keys, ((1,), (1,))) + mm(q_rope, kr[r], ((1,), (1,)))
            score = jnp.where(position < len_ref[0, r], score * SCALING, -jnp.inf)
            top = jnp.max(score, axis=1, keepdims=True)
            lat32, rope32 = q_lat.astype(F32), q_rope.astype(F32)
            news = []
            for t in range(STEPS):
                tok_r = toks[t, pl.ds(r, 1), :]
                new = jnp.sum(lat32 * tok_r[:, :LAT], axis=1, keepdims=True)
                new = new + jnp.sum(rope32 * tok_r[:, LAT:], axis=1, keepdims=True)
                new = new * SCALING
                if t == 1:
                    new = jnp.where(late, new, -jnp.inf)
                news.append((new, tok_r[:, :LAT]))
            for new, _ in news:
                top = jnp.maximum(top, new)
            expped = jnp.exp(score - top)
            new_exp = [jnp.exp(new - top) for new, _ in news]
            total = jnp.sum(expped, axis=1, keepdims=True)
            for e in new_exp:
                total = total + e
            inverse = 1.0 / total
            out = mm((expped * inverse).astype(BF), keys)
            for e, (_, tok_r) in zip(new_exp, news):
                out = out + (e * inverse).astype(BF).astype(F32) * tok_r
            out = out.astype(BF)
            for s in range(STEPS):
                for hh in range(2):
                    first = 16 * (2 * s + hh)
                    attr[hh, 8 * s + i] = out[first : first + 16]
            return carry

        lax.fori_loop(0, 8, attend_row, 0, unroll=4)
        for hh in range(2):
            turned = mm(perm[...], attr[hh].reshape(256, LAT)).astype(BF)
            ab[p, hh] = turned.reshape(2, 8, 16, LAT)
        each_kin(lambda j: back_copy(p, j).start())
        for hh in range(2):
            for f in range(2):
                ar[p, hh, f, rows16(mine), :] = ab[p, hh, f, mine]

    def heads_out(p):
        def back_arrived(j):
            m, t = kin(8 - j)
            there = ar.at[p, :, :, rows16(m), :]
            rcopy(there, there, asend.at[p, j], arecv.at[p, m], tp=t).wait_recv()

        each_kin(back_arrived)
        for f in range(2):
            for hh in range(2):
                first = 256 * f + VDIM * hh
                ho[p, :, first : first + VDIM] = mm(
                    ar[p, hh, f], vm[f, :, hh * VDIM : (hh + 1) * VDIM]
                ).astype(BF)
        for dy in (1, 2, 3):
            gather_copy(p, dy).start()
        hg[p, 0] = ho[p]

    def multiply(p):
        for dy in (1, 2, 3):
            src = rem(y + dy, YS)
            there = hg.at[p, dy]
            rcopy(there, there, hsend.at[p, dy], hrecv.at[p, dy], tp=src * ZS + z).wait_recv()
        for q in (2 * p, 2 * p + 1):
            for first, width in ((0, 512), (512, 384)):
                cols = slice(HALF * (q % 2) + first, HALF * (q % 2) + first + width)
                total = mm(hg[p, 0], wp[0, :, cols])
                for k in range(1, YS):
                    total = total + mm(hg[p, k], wp[k, :, cols])
                pb[q, :, :, :, first : first + width] = total.astype(BF).reshape(YS, 2, 16, width)
            each_kin(lambda j: home_copy(q, j).start())
            hl[q, y, par] = pb[q, y, par]

    def home_arrived(q, j):
        m, t = kin(8 - j)
        there = hl.at[q, div(m, 2), rem(m, 2)]
        rcopy(there, there, fsend.at[q, j], frecv.at[q, m], tp=t).wait_recv()

    attend(0)
    value_copy().start()
    share_weights(0)
    attend(1)
    share_weights(1)
    value_copy().wait_recv()
    heads_out(0)
    heads_out(1)
    load_w.wait()
    for f in range(2):
        weights_arrived(f)
    multiply(0)
    multiply(1)

    for q in range(CHUNKS):
        each_kin(lambda j: home_arrived(q, j))
    for side_cols in range(2):
        for yy in range(YS):
            first = COLS * yy + HALF * side_cols
            top, low = (
                hl[q, yy, 0].astype(F32) + hl[q, yy, 1].astype(F32) for q in (side_cols, 2 + side_cols)
            )
            for s in range(STEPS):
                rows = slice(8 * s, 8 * s + 8)
                both = jnp.concatenate([top[rows], low[rows]], axis=0)
                dec[s, 0, :, first : first + HALF] = both.astype(BF)

    for copy in sent:
        copy.wait_send()
    each(lambda k: pick_copy(k).wait_send())
    swap_bucket().wait_send()
    each(lambda k: rope_copy(k).wait_send())
    for f in range(2):
        for dy in range(1 - f, YS):
            weight_copy(f, dy).wait_send()
        for dx in range(4):
            if dx > 0:
                spread_copy(f, dx).wait_send()
            core_copy(f, dx).wait_send()
    value_copy().wait_send()
    for p in range(PARTS):
        each(lambda k: query_copy(p, k).wait_send())
        each_kin(lambda j: back_copy(p, j).wait_send())
        for dy in (1, 2, 3):
            gather_copy(p, dy).wait_send()
    for q in range(CHUNKS):
        each_kin(lambda j: home_copy(q, j).wait_send())


def hand_over(*refs):
    for source, result in zip(refs[:3], refs[3:]):
        result[...] = source[...]


def local(
    trainer_weight,
    bucket_slot,
    bucket_version,
    replica_version,
    old_weight,
    old_scale,
    q_nope,
    q_rope,
    cache_latent,
    cache_rope,
    new_token,
    lengths,
    out_weight,
):
    dma = pltpu.SemaphoreType.DMA
    results = pl.pallas_call(
        everything,
        out_shape=(
            jax.ShapeDtypeStruct((1, LAT, 512), BF),
            jax.ShapeDtypeStruct((1, 4, 4), F32),
            jax.ShapeDtypeStruct((STEPS, 1, 16, D), BF),
        ),
        in_specs=[SM] * 5 + [HB] * 8,
        out_specs=(VM, VM, VM),
        scratch_shapes=[
            pltpu.VMEM((HEADS, 32, 256), BF),
            pltpu.VMEM((TP, 32, 256), BF),
            pltpu.VMEM((2, LAT, 256), BF),
            pltpu.VMEM((LAT, 512), BF),
            pltpu.VMEM((LAT, 256), BF),
            pltpu.VMEM((2, LAT, 256), BF),
            pltpu.VMEM((STEPS, 256, 256), BF),
            pltpu.VMEM((PARTS, 256, 256), BF),
            pltpu.VMEM((ROWS_DEV, LEN * ROPE), BF),
            pltpu.VMEM((STEPS, ROWS_DEV, LAT + ROPE), BF),
            pltpu.VMEM((ROWS_DEV, LEN, LAT), BF),
            pltpu.VMEM((YS, 512, COLS), BF),
            pltpu.VMEM((256, 256), BF),
            pltpu.VMEM((ROWS_DEV, LEN // 2, 128), BF),
            pltpu.VMEM((ROWS_DEV, LEN, 128), BF),
            pltpu.VMEM((STEPS, ROWS_DEV, 640), F32),
            pltpu.VMEM((PARTS, 2, 256, LAT), BF),
            pltpu.VMEM((PARTS, 2, TP, 16, LAT), BF),
            pltpu.VMEM((STEPS, TP, 16, 128), BF),
            pltpu.VMEM((8, 2 * HEADS, LAT), BF),
            pltpu.VMEM((ROWS_DEV, 2 * HEADS, 128), BF),
            pltpu.VMEM((2, 16, 16, LAT), BF),
            pltpu.VMEM((PARTS, 2, 2, 8, 16, LAT), BF),
            pltpu.VMEM((PARTS, 2, 2, 128, LAT), BF),
            pltpu.VMEM((PARTS, 128, 512), BF),
            pltpu.VMEM((PARTS, YS, 128, 512), BF),
            pltpu.VMEM((CHUNKS, YS, 2, 16, HALF), BF),
            pltpu.VMEM((CHUNKS, YS, 2, 16, HALF), BF),
            dma((8,)),
            dma((15,)),
            dma((REPS,)),
            dma((TP,)),
            dma((TP,)),
            dma(()),
            dma(()),
            dma((2, YS)),
            dma((2, YS)),
            dma((2, 4)),
            dma((2, 4)),
            dma((2, 4)),
            dma((2, 4)),
            dma(()),
            dma(()),
            dma((TP,)),
            dma((TP,)),
            dma((PARTS, TP)),
            dma((PARTS, TP)),
            dma((PARTS, 8)),
            dma((PARTS, 8)),
            dma((PARTS, YS)),
            dma((PARTS, YS)),
            dma((CHUNKS, 8)),
            dma((CHUNKS, 8)),
        ],
        compiler_params=pltpu.CompilerParams(
            collective_id=0, has_side_effects=True, vmem_limit_bytes=56 * 2**20
        ),
        name="push_and_decode",
    )(
        bucket_slot,
        bucket_version,
        replica_version,
        old_scale,
        lengths,
        trainer_weight,
        old_weight,
        q_nope,
        q_rope,
        cache_latent,
        cache_rope,
        new_token,
        out_weight,
    )
    return pl.pallas_call(
        hand_over,
        out_shape=tuple(jax.ShapeDtypeStruct(r.shape, r.dtype) for r in results),
        in_specs=[VM] * 3,
        out_specs=(VM,) * 3,
        compiler_params=pltpu.CompilerParams(vmem_limit_bytes=56 * 2**20),
        name="hand_over",
    )(*results)


def solution(mesh):
    return jax.shard_map(
        local,
        mesh=mesh,
        in_specs=(
            P("rep", "tp", None),
            P(),
            P(),
            P("rep", None),
            P("rep", None, "tp"),
            P("rep", None, "tp"),
            P(None, "rep", None, "tp"),
            P(None, "rep", None, "tp"),
            P("rep", "tp", None, None),
            P("rep", "tp", None),
            P(None, "rep", "tp", None),
            P("rep", "tp"),
            P("tp", None),
        ),
        out_specs=(P("rep", None, "tp"), P("rep", None, "tp"), P(None, "rep", "tp", None)),
        check_vma=False,
    )
```

```python
import jax
import jax.numpy as jnp
from jax import lax
from jax.experimental import pallas as pl
from jax.experimental.pallas import tpu as pltpu
from jax.sharding import PartitionSpec as P

HEADS = 32
LAT = 512
NOPE = 128
ROPE = 64
VDIM = 128
BLOCK = 128
STEPS = 2
PARTS = 2
D = 7168
LEN = 384
YS = 4
ZS = 4
TP = YS * ZS
REPS = 16
ROWS_DEV = 16
COLS = D // YS
HALF = COLS // 2
CHUNKS = 4
EPSILON = 1e-06
SCALING = (NOPE + ROPE) ** (-0.5)
MESH = pl.DeviceIdType.MESH
BF = jnp.bfloat16
F32 = jnp.float32
VM = pl.BlockSpec(memory_space=pltpu.VMEM)
SM = pl.BlockSpec(memory_space=pltpu.SMEM)
HB = pl.BlockSpec(memory_space=pltpu.HBM)


def rem(a, b):
    return lax.rem(a, jnp.int32(b))


def div(a, b):
    return lax.div(a, jnp.int32(b))


def rcopy(src, dst, send_sem, recv_sem, **where):
    return pltpu.make_async_remote_copy(
        src_ref=src,
        dst_ref=dst,
        send_sem=send_sem,
        recv_sem=recv_sem,
        device_id=where,
        device_id_type=MESH,
    )


def greet(peers):
    barrier = pltpu.get_barrier_semaphore()
    for peer in peers:
        pl.semaphore_signal(barrier, inc=1, device_id=peer, device_id_type=MESH)
    pl.semaphore_wait(barrier, len(peers))


def mm(a, b, contract=((1,), (0,))):
    return lax.dot_general(a, b, (contract, ((), ())), preferred_element_type=F32)


def everything(
    slot_ref,
    bver_ref,
    rver_ref,
    oscale_ref,
    len_ref,
    tw_hbm,
    ow_hbm,
    qn_hbm,
    qp_hbm,
    cache_hbm,
    rope_hbm,
    tok_hbm,
    weight_hbm,
    sw_ref,
    ss_ref,
    dec,
    gath,
    sel,
    buck,
    ow,
    km,
    vm,
    qn,
    qn2,
    rope,
    tok,
    cache,
    wp,
    perm,
    ropes,
    kr,
    toks,
    qs,
    qr,
    qrr,
    qrow,
    qro,
    attr,
    ab,
    ar,
    ho,
    hg,
    pb,
    hl,
    lsem,
    gsend,
    grecv,
    tsend,
    trecv,
    csend,
    crecv,
    wsend,
    wrecv,
    xsend,
    xrecv,
    dsend,
    drecv,
    vsend,
    vrecv,
    psend,
    precv,
    qsend,
    qrecv,
    asend,
    arecv,
    hsend,
    hrecv,
    fsend,
    frecv,
):
    rep, tp = lax.axis_index("rep"), lax.axis_index("tp")
    zh, x, c = div(rep, 8), rem(div(rep, 2), 4), rem(rep, 2)
    y, z = div(tp, ZS), rem(tp, ZS)
    zpeer = rem(rep + 8, 16)
    cpeer = rep + 1 - 2 * c
    xpeers = [zh * 8 + rem(x + dx, 4) * 2 + c for dx in (1, 2, 3)]
    far = rem(z + 2, ZS)
    side, par = div(z, 2), rem(z, 2)
    mine = 2 * y + par
    share = 2 * x + c

    def rows16(t):
        return pl.ds(pl.multiple_of(16 * t, 16), 16)

    def rows32(t):
        return pl.ds(pl.multiple_of(32 * t, 32), 32)

    def columns(yy):
        return pl.ds(pl.multiple_of(COLS * yy, 256), COLS)

    def each(fn):
        def body(k, carry):
            fn(k)
            return carry

        lax.fori_loop(1, TP, body, 0)

    def source(k):
        return rem(tp + TP - k, TP)

    def slot_at(owner, reader_side):
        oz = rem(owner, ZS)
        return 8 * rem(div(oz, 2) + reader_side, 2) + 2 * div(owner, ZS) + rem(oz, 2)

    def kin(j):
        m = rem(mine + j, 8)
        return m, div(m, 2) * ZS + 2 * side + rem(m, 2)

    def each_kin(fn):
        def body(j, carry):
            fn(j)
            return carry

        lax.fori_loop(1, 8, body, 0)

    loads = [
        pltpu.make_async_copy(src, dst, lsem.at[i])
        for i, (src, dst) in enumerate(
            [
                (tw_hbm, gath.at[pl.ds(2 * rep, 2)]),
                (qp_hbm.at[:, 0, rows16(tp), :], qrr.at[:, mine]),
                (tok_hbm.at[:, 0], tok),
                (rope_hbm.at[0], rope),
                (ow_hbm.at[0], ow),
                (qn_hbm.at[:, 0], qn),
                (cache_hbm.at[0], cache),
                (weight_hbm.at[:, columns(y)], wp.at[0, pl.ds(0, 256), :]),
            ]
        )
    ]
    load_tw, load_qp, load_tok, load_rope, load_ow, load_qn, load_cache, load_w = loads
    for copy in loads:
        copy.start()
    greet(
        [{"tp": rem(tp + k, TP)} for k in range(1, TP)]
        + [{"rep": r} for r in xpeers + [zpeer, cpeer]]
        + [{"rep": zpeer, "tp": yy * ZS + far} for yy in range(YS)]
    )

    def block(b):
        return gath.at[pl.ds(2 * b, 2)]

    sent = []

    def pass_on(src, b, to):
        copy = rcopy(src, block(b), gsend.at[len(sent)], grecv.at[b], rep=to)
        copy.start()
        sent.append(copy)

    def arrived(b):
        rcopy(block(b), block(b), gsend.at[0], grecv.at[b], rep=zpeer).wait_recv()

    def part(src):
        return buck.at[c, rows32(src), :]

    def pick_copy(k):
        t = rem(tp + k, TP)
        return rcopy(sel.at[k], part(tp), tsend.at[k], trecv.at[tp], tp=t)

    def swap_bucket():
        return rcopy(buck.at[c], buck.at[c], csend, crecv, rep=cpeer)

    def eighth(f, who):
        return pl.ds(pl.multiple_of(256 * f + 32 * who, 32), 32)

    def eighths(f, who):
        return wp.at[pl.ds(1 - f, 3 + f), eighth(f, who), :]

    own_eighth = pl.ds(pl.multiple_of(32 * share, 32), 32)

    def weight_copy(f, dy):
        yy = rem(y + dy, YS)
        src = weight_hbm.at[own_eighth, columns(yy)]
        there = wp.at[(YS - dy) % YS, eighth(f, share), :]
        if f == 0:
            return rcopy(src, there, wsend.at[f, dy], wrecv.at[f, (YS - dy) % YS], tp=yy * ZS + z)
        to = rem(rep + 8 * (1 - c), 16)
        return rcopy(src, there, wsend.at[f, dy], wrecv.at[f, (YS - dy) % YS], rep=to, tp=yy * ZS + far)

    def spread_copy(f, dx):
        here = eighths(f, share)
        return rcopy(here, here, xsend.at[f, dx], xrecv.at[f, x], rep=xpeers[dx - 1])

    def core_copy(f, dx):
        xx = rem(x + dx, 4)
        here = eighths(f, 2 * xx + c)
        return rcopy(here, here, dsend.at[f, dx], drecv.at[f, xx], rep=cpeer)

    def spread_weights(f):
        for j in range(1 - f, YS):
            there = wp.at[j, eighth(f, share), :]
            rcopy(there, there, wsend.at[f, j], wrecv.at[f, j], rep=cpeer).wait_recv()
        for dx in (2, 1, 3):
            spread_copy(f, dx).start()
        core_copy(f, 0).start()

    def share_weights(f):
        for dx in (1, 3, 2):
            xx = rem(x + dx, 4)
            there = eighths(f, 2 * xx + c)
            rcopy(there, there, xsend.at[f, dx], xrecv.at[f, xx], rep=cpeer).wait_recv()
            core_copy(f, dx).start()

    def weights_arrived(f):
        for xx in range(4):
            there = eighths(f, 2 * xx + 1 - c)
            rcopy(there, there, dsend.at[f, 0], drecv.at[f, xx], rep=cpeer).wait_recv()

    def value_copy():
        return rcopy(vm.at[0], vm.at[1], vsend, vrecv, tp=y * ZS + far)

    def rope_copy(k):
        t = rem(tp + k, TP)
        there = qrr.at[:, slot_at(tp, div(rem(t, ZS), 2))]
        return rcopy(qp_hbm.at[:, 0, rows16(t), :], there, psend.at[k], precv.at[tp], tp=t)

    def query_copy(p, k):
        t = rem(tp + k, TP)
        there = qr.at[p, :, slot_at(tp, div(rem(t, ZS), 2))]
        return rcopy(qs.at[p, :, rows16(t), :], there, qsend.at[p, k], qrecv.at[p, tp], tp=t)

    def back_copy(p, j):
        m, t = kin(j)
        there = ar.at[p, :, :, rows16(mine), :]
        return rcopy(ab.at[p, :, :, m], there, asend.at[p, j], arecv.at[p, mine], tp=t)

    def gather_copy(p, dy):
        to = rem(y + dy, YS) * ZS + z
        return rcopy(ho.at[p], hg.at[p, YS - dy], hsend.at[p, dy], hrecv.at[p, YS - dy], tp=to)

    def home_copy(q, j):
        m, t = kin(j)
        there = hl.at[q, y, par]
        return rcopy(pb.at[q, div(m, 2), rem(m, 2)], there, fsend.at[q, j], frecv.at[q, mine], tp=t)

    for to in [zpeer] + xpeers + [cpeer]:
        pass_on(tw_hbm, rep, to)
    for dy in range(YS):
        weight_copy(1, dy).start()
    arrived(zpeer)
    for to in xpeers + [cpeer]:
        pass_on(block(zpeer), zpeer, to)
    for dy in (2, 1, 3):
        weight_copy(0, dy).start()
    for xp in xpeers:
        arrived(xp)
        pass_on(block(xp), xp, cpeer)
    for xp in xpeers:
        b = rem(xp + 8, 16)
        arrived(b)
        pass_on(block(b), b, cpeer)
    load_tw.wait()
    for b in [zpeer, rep] + xpeers + [rem(xp + 8, 16) for xp in xpeers]:
        arrived(b + 1 - 2 * c)

    def pick(k):
        sel[k] = gath[slot_ref[2 * rem(tp + k, TP) + c]]
        pick_copy(k).start()

    each(pick)
    buck[c, rows32(tp), :] = gath[slot_ref[2 * tp + c]]
    spread_weights(0)
    each(lambda k: rope_copy(k).start())

    pi = lax.broadcasted_iota(jnp.int32, (256, 256), 0)
    pj = lax.broadcasted_iota(jnp.int32, (256, 256), 1)
    swapped = ((pi >> 4) == (pj & 15)) & ((pi & 15) == (pj >> 4))
    perm[...] = jnp.where(swapped, 1.0, 0.0).astype(BF)
    load_tok.wait()
    toks[...] = jnp.zeros_like(toks)
    toks[:, :, 0 : LAT + ROPE] = tok[...].astype(F32)
    load_rope.wait()
    for g in range(12):
        tiles = [rope[:, (16 * g + i) * 128 : (16 * g + i + 1) * 128] for i in range(16)]
        turned = mm(perm[...], jnp.concatenate(tiles, axis=0)).astype(BF)
        ropes[:, 16 * g : 16 * (g + 1), :] = turned.reshape(16, 16, 128)

    load_qn.wait()

    def reorder(t, carry):
        first = qn[0, rows16(t), :].astype(F32)
        second = qn[1, rows16(t), :].astype(F32)
        for p in range(PARTS):
            rows = slice(8 * p, 8 * p + 8)
            both = jnp.concatenate([first[rows], second[rows]], axis=0)
            qn2[p, rows16(t), :] = both.astype(BF)
        return carry

    lax.fori_loop(0, TP, reorder, 0)

    load_ow.wait()

    def bucket_arrived(k):
        src = source(k)
        rcopy(part(src), part(src), tsend.at[k], trecv.at[src], tp=src).wait_recv()

    each(bucket_arrived)
    swap_bucket().start()
    there = buck.at[1 - c]
    rcopy(there, there, csend, crecv, rep=cpeer).wait_recv()

    cell_row = lax.broadcasted_iota(jnp.int32, (4, 4), 0)
    cell_col = lax.broadcasted_iota(jnp.int32, (4, 4), 1)

    def serve(hh, cc, scales):
        head = 2 * tp + hh
        stale = (rver_ref[0, head] != bver_ref[head]).astype(jnp.int32)
        col = hh * 256 + cc * BLOCK
        for i in range(4):
            rows = slice(i * BLOCK, (i + 1) * BLOCK)
            raw = buck[hh, rows, cc * BLOCK : (cc + 1) * BLOCK].astype(F32)
            peak = jnp.max(jnp.abs(raw), axis=0, keepdims=True)
            peak = jnp.max(peak, axis=1, keepdims=True)
            scale = peak + EPSILON
            fresh = (raw / scale).astype(BF).astype(F32)
            old = ow[rows, col : col + BLOCK].astype(F32)
            served = jnp.where(jnp.zeros((BLOCK, BLOCK), jnp.int32) + stale != 0, fresh, old)
            held = jnp.zeros((1, 1), F32) + oscale_ref[0, i, 2 * hh + cc]
            used = jnp.where(jnp.zeros((1, 1), jnp.int32) + stale != 0, scale, held)
            sw_ref[0, rows, col : col + BLOCK] = served.astype(BF)
            maps = km if cc == 0 else vm.at[0]
            maps[rows, hh * BLOCK : (hh + 1) * BLOCK] = (served * used).astype(BF)
            here = (cell_row == i) & (cell_col == 2 * hh + cc)
            scales = jnp.where(here, used, scales)
        return scales

    scales = jnp.zeros((4, 4), F32)
    for hh in range(2):
        scales = serve(hh, 0, scales)

    for p in range(PARTS):
        for hh in range(2):
            qs[p, hh] = mm(
                qn2[p, :, hh * NOPE : (hh + 1) * NOPE],
                km[:, hh * BLOCK : (hh + 1) * BLOCK],
                ((1,), (1,)),
            ).astype(BF)
        each(lambda k: query_copy(p, k).start())
    spread_weights(1)
    for hh in range(2):
        scales = serve(hh, 1, scales)
    ss_ref[0] = scales
    for p in range(PARTS):
        for hh in range(2):
            qr[p, hh, mine] = qs[p, hh, rows16(tp), :]

    si = lax.broadcasted_iota(jnp.int32, (LEN, LEN // 2), 0)
    sj = lax.broadcasted_iota(jnp.int32, (LEN, LEN // 2), 1)
    spread = jnp.where((si >> 1) == sj, 1.0, 0.0).astype(BF)
    ki = lax.broadcasted_iota(jnp.int32, (LEN, 128), 0)
    kj = lax.broadcasted_iota(jnp.int32, (LEN, 128), 1)
    kept = (ki & 1) == (kj >> 6)

    def place(r, carry):
        kr[r] = jnp.where(kept, mm(spread, ropes[r]), 0.0).astype(BF)
        return carry

    lax.fori_loop(0, ROWS_DEV, place, 0)
    load_cache.wait()
    load_qp.wait()

    di = lax.broadcasted_iota(jnp.int32, (128, 256), 0)
    dj = lax.broadcasted_iota(jnp.int32, (128, 256), 1)
    double = jnp.where(di == (dj >> 7) * 64 + (dj & 63), 1.0, 0.0).astype(BF)
    position = lax.broadcasted_iota(jnp.int32, (1, LEN), 1)

    def rope_arrived(k):
        src = source(k)
        there = qrr.at[:, slot_at(src, side)]
        rcopy(there, there, psend.at[k], precv.at[src], tp=src).wait_recv()

    each(rope_arrived)
    for s in range(STEPS):
        turned = mm(perm[...], qrr[s].reshape(256, 128)).astype(BF)
        turned = mm(turned, double).astype(BF)
        for hh in range(2):
            first = 16 * (2 * s + hh)
            qro[:, first : first + 16, :] = turned[:, 128 * hh : 128 * (hh + 1)].reshape(16, 16, 128)
    late = lax.broadcasted_iota(jnp.int32, (2 * HEADS, 1), 0) >= HEADS

    def attend(p):
        def query_arrived(k):
            src = source(k)
            there = qr.at[p, :, slot_at(src, side)]
            rcopy(there, there, qsend.at[p, k], qrecv.at[p, src], tp=src).wait_recv()

        each(query_arrived)
        for hh in range(2):
            turned = mm(perm[...], qr[p, hh].reshape(256, LAT)).astype(BF)
            turned = turned.reshape(2, 8, 16, LAT)
            for s in range(STEPS):
                first = 16 * (2 * s + hh)
                qrow[:, first : first + 16, :] = turned[s]

        def attend_row(i, carry):
            r = 8 * p + i
            q_lat, q_rope, keys = qrow[i], qro[r], cache[r]
            score = mm(q_lat, keys, ((1,), (1,))) + mm(q_rope, kr[r], ((1,), (1,)))
            score = jnp.where(position < len_ref[0, r], score * SCALING, -jnp.inf)
            top = jnp.max(score, axis=1, keepdims=True)
            lat32, rope32 = q_lat.astype(F32), q_rope.astype(F32)
            news = []
            for t in range(STEPS):
                tok_r = toks[t, pl.ds(r, 1), :]
                new = jnp.sum(lat32 * tok_r[:, :LAT], axis=1, keepdims=True)
                new = new + jnp.sum(rope32 * tok_r[:, LAT:], axis=1, keepdims=True)
                new = new * SCALING
                if t == 1:
                    new = jnp.where(late, new, -jnp.inf)
                news.append((new, tok_r[:, :LAT]))
            for new, _ in news:
                top = jnp.maximum(top, new)
            expped = jnp.exp(score - top)
            new_exp = [jnp.exp(new - top) for new, _ in news]
            total = jnp.sum(expped, axis=1, keepdims=True)
            for e in new_exp:
                total = total + e
            inverse = 1.0 / total
            out = mm((expped * inverse).astype(BF), keys)
            for e, (_, tok_r) in zip(new_exp, news):
                out = out + (e * inverse).astype(BF).astype(F32) * tok_r
            out = out.astype(BF)
            for s in range(STEPS):
                for hh in range(2):
                    first = 16 * (2 * s + hh)
                    attr[hh, 8 * s + i] = out[first : first + 16]
            return carry

        lax.fori_loop(0, 8, attend_row, 0, unroll=4)
        for hh in range(2):
            turned = mm(perm[...], attr[hh].reshape(256, LAT)).astype(BF)
            ab[p, hh] = turned.reshape(2, 8, 16, LAT)
        each_kin(lambda j: back_copy(p, j).start())
        for hh in range(2):
            for f in range(2):
                ar[p, hh, f, rows16(mine), :] = ab[p, hh, f, mine]

    def heads_out(p):
        def back_arrived(j):
            m, t = kin(8 - j)
            there = ar.at[p, :, :, rows16(m), :]
            rcopy(there, there, asend.at[p, j], arecv.at[p, m], tp=t).wait_recv()

        each_kin(back_arrived)
        for f in range(2):
            for hh in range(2):
                first = 256 * f + VDIM * hh
                ho[p, :, first : first + VDIM] = mm(
                    ar[p, hh, f], vm[f, :, hh * VDIM : (hh + 1) * VDIM]
                ).astype(BF)
        for dy in (1, 2, 3):
            gather_copy(p, dy).start()
        hg[p, 0] = ho[p]

    def multiply(p):
        for dy in (1, 2, 3):
            src = rem(y + dy, YS)
            there = hg.at[p, dy]
            rcopy(there, there, hsend.at[p, dy], hrecv.at[p, dy], tp=src * ZS + z).wait_recv()
        for q in (2 * p, 2 * p + 1):
            for first, width in ((0, 512), (512, 384)):
                cols = slice(HALF * (q % 2) + first, HALF * (q % 2) + first + width)
                total = mm(hg[p, 0], wp[0, :, cols])
                for k in range(1, YS):
                    total = total + mm(hg[p, k], wp[k, :, cols])
                pb[q, :, :, :, first : first + width] = total.astype(BF).reshape(YS, 2, 16, width)
            each_kin(lambda j: home_copy(q, j).start())
            hl[q, y, par] = pb[q, y, par]

    def home_arrived(q, j):
        m, t = kin(8 - j)
        there = hl.at[q, div(m, 2), rem(m, 2)]
        rcopy(there, there, fsend.at[q, j], frecv.at[q, m], tp=t).wait_recv()

    attend(0)
    value_copy().start()
    share_weights(0)
    attend(1)
    share_weights(1)
    value_copy().wait_recv()
    heads_out(0)
    heads_out(1)
    load_w.wait()
    for f in range(2):
        weights_arrived(f)
    multiply(0)
    multiply(1)

    for q in range(CHUNKS):
        each_kin(lambda j: home_arrived(q, j))
    for side_cols in range(2):
        for yy in range(YS):
            first = COLS * yy + HALF * side_cols
            top, low = (
                hl[q, yy, 0].astype(F32) + hl[q, yy, 1].astype(F32) for q in (side_cols, 2 + side_cols)
            )
            for s in range(STEPS):
                rows = slice(8 * s, 8 * s + 8)
                both = jnp.concatenate([top[rows], low[rows]], axis=0)
                dec[s, 0, :, first : first + HALF] = both.astype(BF)

    for copy in sent:
        copy.wait_send()
    each(lambda k: pick_copy(k).wait_send())
    swap_bucket().wait_send()
    each(lambda k: rope_copy(k).wait_send())
    for f in range(2):
        for dy in range(1 - f, YS):
            weight_copy(f, dy).wait_send()
        for dx in range(4):
            if dx > 0:
                spread_copy(f, dx).wait_send()
            core_copy(f, dx).wait_send()
    value_copy().wait_send()
    for p in range(PARTS):
        each(lambda k: query_copy(p, k).wait_send())
        each_kin(lambda j: back_copy(p, j).wait_send())
        for dy in (1, 2, 3):
            gather_copy(p, dy).wait_send()
    for q in range(CHUNKS):
        each_kin(lambda j: home_copy(q, j).wait_send())


def hand_over(*refs):
    for source, result in zip(refs[:3], refs[3:]):
        result[...] = source[...]


def local(
    trainer_weight,
    bucket_slot,
    bucket_version,
    replica_version,
    old_weight,
    old_scale,
    q_nope,
    q_rope,
    cache_latent,
    cache_rope,
    new_token,
    lengths,
    out_weight,
):
    dma = pltpu.SemaphoreType.DMA
    results = pl.pallas_call(
        everything,
        out_shape=(
            jax.ShapeDtypeStruct((1, LAT, 512), BF),
            jax.ShapeDtypeStruct((1, 4, 4), F32),
            jax.ShapeDtypeStruct((STEPS, 1, 16, D), BF),
        ),
        in_specs=[SM] * 5 + [HB] * 8,
        out_specs=(VM, VM, VM),
        scratch_shapes=[
            pltpu.VMEM((HEADS, 32, 256), BF),
            pltpu.VMEM((TP, 32, 256), BF),
            pltpu.VMEM((2, LAT, 256), BF),
            pltpu.VMEM((LAT, 512), BF),
            pltpu.VMEM((LAT, 256), BF),
            pltpu.VMEM((2, LAT, 256), BF),
            pltpu.VMEM((STEPS, 256, 256), BF),
            pltpu.VMEM((PARTS, 256, 256), BF),
            pltpu.VMEM((ROWS_DEV, LEN * ROPE), BF),
            pltpu.VMEM((STEPS, ROWS_DEV, LAT + ROPE), BF),
            pltpu.VMEM((ROWS_DEV, LEN, LAT), BF),
            pltpu.VMEM((YS, 512, COLS), BF),
            pltpu.VMEM((256, 256), BF),
            pltpu.VMEM((ROWS_DEV, LEN // 2, 128), BF),
            pltpu.VMEM((ROWS_DEV, LEN, 128), BF),
            pltpu.VMEM((STEPS, ROWS_DEV, 640), F32),
            pltpu.VMEM((PARTS, 2, 256, LAT), BF),
            pltpu.VMEM((PARTS, 2, TP, 16, LAT), BF),
            pltpu.VMEM((STEPS, TP, 16, 128), BF),
            pltpu.VMEM((8, 2 * HEADS, LAT), BF),
            pltpu.VMEM((ROWS_DEV, 2 * HEADS, 128), BF),
            pltpu.VMEM((2, 16, 16, LAT), BF),
            pltpu.VMEM((PARTS, 2, 2, 8, 16, LAT), BF),
            pltpu.VMEM((PARTS, 2, 2, 128, LAT), BF),
            pltpu.VMEM((PARTS, 128, 512), BF),
            pltpu.VMEM((PARTS, YS, 128, 512), BF),
            pltpu.VMEM((CHUNKS, YS, 2, 16, HALF), BF),
            pltpu.VMEM((CHUNKS, YS, 2, 16, HALF), BF),
            dma((8,)),
            dma((15,)),
            dma((REPS,)),
            dma((TP,)),
            dma((TP,)),
            dma(()),
            dma(()),
            dma((2, YS)),
            dma((2, YS)),
            dma((2, 4)),
            dma((2, 4)),
            dma((2, 4)),
            dma((2, 4)),
            dma(()),
            dma(()),
            dma((TP,)),
            dma((TP,)),
            dma((PARTS, TP)),
            dma((PARTS, TP)),
            dma((PARTS, 8)),
            dma((PARTS, 8)),
            dma((PARTS, YS)),
            dma((PARTS, YS)),
            dma((CHUNKS, 8)),
            dma((CHUNKS, 8)),
        ],
        compiler_params=pltpu.CompilerParams(
            collective_id=0, has_side_effects=True, vmem_limit_bytes=56 * 2**20
        ),
        name="push_and_decode",
    )(
        bucket_slot,
        bucket_version,
        replica_version,
        old_scale,
        lengths,
        trainer_weight,
        old_weight,
        q_nope,
        q_rope,
        cache_latent,
        cache_rope,
        new_token,
        out_weight,
    )
    return pl.pallas_call(
        hand_over,
        out_shape=tuple(jax.ShapeDtypeStruct(r.shape, r.dtype) for r in results),
        in_specs=[VM] * 3,
        out_specs=(VM,) * 3,
        compiler_params=pltpu.CompilerParams(vmem_limit_bytes=56 * 2**20),
        name="hand_over",
    )(*results)


def solution(mesh):
    return jax.shard_map(
        local,
        mesh=mesh,
        in_specs=(
            P("rep", "tp", None),
            P(),
            P(),
            P("rep", None),
            P("rep", None, "tp"),
            P("rep", None, "tp"),
            P(None, "rep", None, "tp"),
            P(None, "rep", None, "tp"),
            P("rep", "tp", None, None),
            P("rep", "tp", None),
            P(None, "rep", "tp", None),
            P("rep", "tp"),
            P("tp", None),
        ),
        out_specs=(P("rep", None, "tp"), P("rep", None, "tp"), P(None, "rep", "tp", None)),
        check_vma=False,
    )
```

```python
import jax
import jax.numpy as jnp
from jax import lax
from jax.experimental import pallas as pl
from jax.experimental.pallas import tpu as pltpu
from jax.sharding import PartitionSpec as P

HEADS = 32
LAT = 512
NOPE = 128
ROPE = 64
VDIM = 128
BLOCK = 128
STEPS = 2
PARTS = 2
D = 7168
LEN = 384
YS = 4
ZS = 4
TP = YS * ZS
REPS = 16
ROWS_DEV = 16
COLS = D // YS
HALF = COLS // 2
CHUNKS = 4
EPSILON = 1e-06
SCALING = (NOPE + ROPE) ** (-0.5)
MESH = pl.DeviceIdType.MESH
BF = jnp.bfloat16
F32 = jnp.float32
VM = pl.BlockSpec(memory_space=pltpu.VMEM)
SM = pl.BlockSpec(memory_space=pltpu.SMEM)
HB = pl.BlockSpec(memory_space=pltpu.HBM)


def rem(a, b):
    return lax.rem(a, jnp.int32(b))


def div(a, b):
    return lax.div(a, jnp.int32(b))


def rcopy(src, dst, send_sem, recv_sem, **where):
    return pltpu.make_async_remote_copy(
        src_ref=src,
        dst_ref=dst,
        send_sem=send_sem,
        recv_sem=recv_sem,
        device_id=where,
        device_id_type=MESH,
    )


def greet(peers):
    barrier = pltpu.get_barrier_semaphore()
    for peer in peers:
        pl.semaphore_signal(barrier, inc=1, device_id=peer, device_id_type=MESH)
    pl.semaphore_wait(barrier, len(peers))


def mm(a, b, contract=((1,), (0,))):
    return lax.dot_general(a, b, (contract, ((), ())), preferred_element_type=F32)


def everything(
    slot_ref,
    bver_ref,
    rver_ref,
    oscale_ref,
    len_ref,
    tw_hbm,
    ow_hbm,
    qn_hbm,
    qp_hbm,
    cache_hbm,
    rope_hbm,
    tok_hbm,
    weight_hbm,
    sw_hbm,
    ss_ref,
    dec,
    served_now,
    gath,
    sel,
    buck,
    ow,
    km,
    vm,
    qn,
    qn2,
    rope,
    tok,
    cache,
    wp,
    perm,
    ropes,
    kr,
    toks,
    qs,
    qr,
    qrr,
    qrow,
    qro,
    attr,
    ab,
    ar,
    ho,
    hg,
    pb,
    hl,
    lsem,
    gsend,
    grecv,
    tsend,
    trecv,
    csend,
    crecv,
    wsend,
    wrecv,
    xsend,
    xrecv,
    dsend,
    drecv,
    vsend,
    vrecv,
    psend,
    precv,
    qsend,
    qrecv,
    asend,
    arecv,
    hsend,
    hrecv,
    fsend,
    frecv,
):
    rep, tp = lax.axis_index("rep"), lax.axis_index("tp")
    zh, x, c = div(rep, 8), rem(div(rep, 2), 4), rem(rep, 2)
    y, z = div(tp, ZS), rem(tp, ZS)
    zpeer = rem(rep + 8, 16)
    cpeer = rep + 1 - 2 * c
    xpeers = [zh * 8 + rem(x + dx, 4) * 2 + c for dx in (1, 2, 3)]
    far = rem(z + 2, ZS)
    side, par = div(z, 2), rem(z, 2)
    mine = 2 * y + par
    share = 2 * x + c

    def rows16(t):
        return pl.ds(pl.multiple_of(16 * t, 16), 16)

    def rows32(t):
        return pl.ds(pl.multiple_of(32 * t, 32), 32)

    def columns(yy):
        return pl.ds(pl.multiple_of(COLS * yy, 256), COLS)

    def each(fn):
        def body(k, carry):
            fn(k)
            return carry

        lax.fori_loop(1, TP, body, 0)

    def source(k):
        return rem(tp + TP - k, TP)

    def slot_at(owner, reader_side):
        oz = rem(owner, ZS)
        return 8 * rem(div(oz, 2) + reader_side, 2) + 2 * div(owner, ZS) + rem(oz, 2)

    def kin(j):
        m = rem(mine + j, 8)
        return m, div(m, 2) * ZS + 2 * side + rem(m, 2)

    def each_kin(fn):
        def body(j, carry):
            fn(j)
            return carry

        lax.fori_loop(1, 8, body, 0)

    loads = [
        pltpu.make_async_copy(src, dst, lsem.at[i])
        for i, (src, dst) in enumerate(
            [
                (tw_hbm, gath.at[pl.ds(2 * rep, 2)]),
                (qp_hbm.at[:, 0, rows16(tp), :], qrr.at[:, mine]),
                (tok_hbm.at[:, 0], tok),
                (rope_hbm.at[0], rope),
                (ow_hbm.at[0], ow),
                (qn_hbm.at[:, 0], qn),
                (cache_hbm.at[0], cache),
                (weight_hbm.at[:, columns(y)], wp.at[0, pl.ds(0, 256), :]),
            ]
        )
    ]
    load_tw, load_qp, load_tok, load_rope, load_ow, load_qn, load_cache, load_w = loads
    for copy in loads:
        copy.start()
    greet(
        [{"tp": rem(tp + k, TP)} for k in range(1, TP)]
        + [{"rep": r} for r in xpeers + [zpeer, cpeer]]
        + [{"rep": zpeer, "tp": yy * ZS + far} for yy in range(YS)]
    )

    def block(b):
        return gath.at[pl.ds(2 * b, 2)]

    sent = []

    def pass_on(src, b, to):
        copy = rcopy(src, block(b), gsend.at[len(sent)], grecv.at[b], rep=to)
        copy.start()
        sent.append(copy)

    def arrived(b):
        rcopy(block(b), block(b), gsend.at[0], grecv.at[b], rep=zpeer).wait_recv()

    def part(src):
        return buck.at[c, rows32(src), :]

    def pick_copy(k):
        t = rem(tp + k, TP)
        return rcopy(sel.at[k], part(tp), tsend.at[k], trecv.at[tp], tp=t)

    def swap_bucket():
        return rcopy(buck.at[c], buck.at[c], csend, crecv, rep=cpeer)

    def eighth(f, who):
        return pl.ds(pl.multiple_of(256 * f + 32 * who, 32), 32)

    def eighths(f, who):
        return wp.at[pl.ds(1 - f, 3 + f), eighth(f, who), :]

    own_eighth = pl.ds(pl.multiple_of(32 * share, 32), 32)

    def weight_copy(f, dy):
        yy = rem(y + dy, YS)
        src = weight_hbm.at[own_eighth, columns(yy)]
        there = wp.at[(YS - dy) % YS, eighth(f, share), :]
        if f == 0:
            return rcopy(src, there, wsend.at[f, dy], wrecv.at[f, (YS - dy) % YS], tp=yy * ZS + z)
        to = rem(rep + 8 * (1 - c), 16)
        return rcopy(src, there, wsend.at[f, dy], wrecv.at[f, (YS - dy) % YS], rep=to, tp=yy * ZS + far)

    def spread_copy(f, dx):
        here = eighths(f, share)
        return rcopy(here, here, xsend.at[f, dx], xrecv.at[f, x], rep=xpeers[dx - 1])

    def core_copy(f, dx):
        xx = rem(x + dx, 4)
        here = eighths(f, 2 * xx + c)
        return rcopy(here, here, dsend.at[f, dx], drecv.at[f, xx], rep=cpeer)

    def spread_weights(f):
        for j in range(1 - f, YS):
            there = wp.at[j, eighth(f, share), :]
            rcopy(there, there, wsend.at[f, j], wrecv.at[f, j], rep=cpeer).wait_recv()
        for dx in (2, 1, 3):
            spread_copy(f, dx).start()
        core_copy(f, 0).start()

    def share_weights(f):
        for dx in (1, 3, 2):
            xx = rem(x + dx, 4)
            there = eighths(f, 2 * xx + c)
            rcopy(there, there, xsend.at[f, dx], xrecv.at[f, xx], rep=cpeer).wait_recv()
            core_copy(f, dx).start()

    def weights_arrived(f):
        for xx in range(4):
            there = eighths(f, 2 * xx + 1 - c)
            rcopy(there, there, dsend.at[f, 0], drecv.at[f, xx], rep=cpeer).wait_recv()

    def value_copy():
        return rcopy(vm.at[0], vm.at[1], vsend, vrecv, tp=y * ZS + far)

    def rope_copy(k):
        t = rem(tp + k, TP)
        there = qrr.at[:, slot_at(tp, div(rem(t, ZS), 2))]
        return rcopy(qp_hbm.at[:, 0, rows16(t), :], there, psend.at[k], precv.at[tp], tp=t)

    def query_copy(p, k):
        t = rem(tp + k, TP)
        there = qr.at[p, :, slot_at(tp, div(rem(t, ZS), 2))]
        return rcopy(qs.at[p, :, rows16(t), :], there, qsend.at[p, k], qrecv.at[p, tp], tp=t)

    def back_copy(p, j):
        m, t = kin(j)
        there = ar.at[p, :, :, rows16(mine), :]
        return rcopy(ab.at[p, :, :, m], there, asend.at[p, j], arecv.at[p, mine], tp=t)

    def gather_copy(p, dy):
        to = rem(y + dy, YS) * ZS + z
        return rcopy(ho.at[p], hg.at[p, YS - dy], hsend.at[p, dy], hrecv.at[p, YS - dy], tp=to)

    def home_copy(q, j):
        m, t = kin(j)
        there = hl.at[q, y, par]
        return rcopy(pb.at[q, div(m, 2), rem(m, 2)], there, fsend.at[q, j], frecv.at[q, mine], tp=t)

    for to in [zpeer] + xpeers + [cpeer]:
        pass_on(tw_hbm, rep, to)
    for dy in range(YS):
        weight_copy(1, dy).start()
    arrived(zpeer)
    for to in xpeers + [cpeer]:
        pass_on(block(zpeer), zpeer, to)
    for dy in (2, 1, 3):
        weight_copy(0, dy).start()
    for xp in xpeers:
        arrived(xp)
        pass_on(block(xp), xp, cpeer)
    for xp in xpeers:
        b = rem(xp + 8, 16)
        arrived(b)
        pass_on(block(b), b, cpeer)
    load_tw.wait()
    for b in [zpeer, rep] + xpeers + [rem(xp + 8, 16) for xp in xpeers]:
        arrived(b + 1 - 2 * c)

    def pick(k):
        sel[k] = gath[slot_ref[2 * rem(tp + k, TP) + c]]
        pick_copy(k).start()

    each(pick)
    buck[c, rows32(tp), :] = gath[slot_ref[2 * tp + c]]
    spread_weights(0)
    each(lambda k: rope_copy(k).start())

    pi = lax.broadcasted_iota(jnp.int32, (256, 256), 0)
    pj = lax.broadcasted_iota(jnp.int32, (256, 256), 1)
    swapped = ((pi >> 4) == (pj & 15)) & ((pi & 15) == (pj >> 4))
    perm[...] = jnp.where(swapped, 1.0, 0.0).astype(BF)
    load_tok.wait()
    toks[...] = jnp.zeros_like(toks)
    toks[:, :, 0 : LAT + ROPE] = tok[...].astype(F32)
    load_rope.wait()
    for g in range(12):
        tiles = [rope[:, (16 * g + i) * 128 : (16 * g + i + 1) * 128] for i in range(16)]
        turned = mm(perm[...], jnp.concatenate(tiles, axis=0)).astype(BF)
        ropes[:, 16 * g : 16 * (g + 1), :] = turned.reshape(16, 16, 128)

    load_qn.wait()

    def reorder(t, carry):
        first = qn[0, rows16(t), :].astype(F32)
        second = qn[1, rows16(t), :].astype(F32)
        for p in range(PARTS):
            rows = slice(8 * p, 8 * p + 8)
            both = jnp.concatenate([first[rows], second[rows]], axis=0)
            qn2[p, rows16(t), :] = both.astype(BF)
        return carry

    lax.fori_loop(0, TP, reorder, 0)

    load_ow.wait()

    def bucket_arrived(k):
        src = source(k)
        rcopy(part(src), part(src), tsend.at[k], trecv.at[src], tp=src).wait_recv()

    each(bucket_arrived)
    swap_bucket().start()
    there = buck.at[1 - c]
    rcopy(there, there, csend, crecv, rep=cpeer).wait_recv()

    cell_row = lax.broadcasted_iota(jnp.int32, (4, 4), 0)
    cell_col = lax.broadcasted_iota(jnp.int32, (4, 4), 1)

    def serve(hh, cc, scales):
        head = 2 * tp + hh
        stale = (rver_ref[0, head] != bver_ref[head]).astype(jnp.int32)
        col = hh * 256 + cc * BLOCK
        for i in range(4):
            rows = slice(i * BLOCK, (i + 1) * BLOCK)
            raw = buck[hh, rows, cc * BLOCK : (cc + 1) * BLOCK].astype(F32)
            peak = jnp.max(jnp.abs(raw), axis=0, keepdims=True)
            peak = jnp.max(peak, axis=1, keepdims=True)
            scale = peak + EPSILON
            fresh = (raw / scale).astype(BF).astype(F32)
            old = ow[rows, col : col + BLOCK].astype(F32)
            served = jnp.where(jnp.zeros((BLOCK, BLOCK), jnp.int32) + stale != 0, fresh, old)
            held = jnp.zeros((1, 1), F32) + oscale_ref[0, i, 2 * hh + cc]
            used = jnp.where(jnp.zeros((1, 1), jnp.int32) + stale != 0, scale, held)
            served_now[rows, col : col + BLOCK] = served.astype(BF)
            maps = km if cc == 0 else vm.at[0]
            maps[rows, hh * BLOCK : (hh + 1) * BLOCK] = (served * used).astype(BF)
            here = (cell_row == i) & (cell_col == 2 * hh + cc)
            scales = jnp.where(here, used, scales)
        return scales

    scales = jnp.zeros((4, 4), F32)
    for hh in range(2):
        scales = serve(hh, 0, scales)

    for p in range(PARTS):
        for hh in range(2):
            qs[p, hh] = mm(
                qn2[p, :, hh * NOPE : (hh + 1) * NOPE],
                km[:, hh * BLOCK : (hh + 1) * BLOCK],
                ((1,), (1,)),
            ).astype(BF)
        each(lambda k: query_copy(p, k).start())
    spread_weights(1)
    for hh in range(2):
        scales = serve(hh, 1, scales)
    ss_ref[0] = scales
    store_served = pltpu.make_async_copy(served_now, sw_hbm.at[0], lsem.at[8])
    store_served.start()
    for p in range(PARTS):
        for hh in range(2):
            qr[p, hh, mine] = qs[p, hh, rows16(tp), :]

    si = lax.broadcasted_iota(jnp.int32, (LEN, LEN // 2), 0)
    sj = lax.broadcasted_iota(jnp.int32, (LEN, LEN // 2), 1)
    spread = jnp.where((si >> 1) == sj, 1.0, 0.0).astype(BF)
    ki = lax.broadcasted_iota(jnp.int32, (LEN, 128), 0)
    kj = lax.broadcasted_iota(jnp.int32, (LEN, 128), 1)
    kept = (ki & 1) == (kj >> 6)

    def place(r, carry):
        kr[r] = jnp.where(kept, mm(spread, ropes[r]), 0.0).astype(BF)
        return carry

    lax.fori_loop(0, ROWS_DEV, place, 0)
    load_cache.wait()
    load_qp.wait()

    di = lax.broadcasted_iota(jnp.int32, (128, 256), 0)
    dj = lax.broadcasted_iota(jnp.int32, (128, 256), 1)
    double = jnp.where(di == (dj >> 7) * 64 + (dj & 63), 1.0, 0.0).astype(BF)
    position = lax.broadcasted_iota(jnp.int32, (1, LEN), 1)

    def rope_arrived(k):
        src = source(k)
        there = qrr.at[:, slot_at(src, side)]
        rcopy(there, there, psend.at[k], precv.at[src], tp=src).wait_recv()

    each(rope_arrived)
    for s in range(STEPS):
        turned = mm(perm[...], qrr[s].reshape(256, 128)).astype(BF)
        turned = mm(turned, double).astype(BF)
        for hh in range(2):
            first = 16 * (2 * s + hh)
            qro[:, first : first + 16, :] = turned[:, 128 * hh : 128 * (hh + 1)].reshape(16, 16, 128)
    late = lax.broadcasted_iota(jnp.int32, (2 * HEADS, 1), 0) >= HEADS

    def attend(p):
        def query_arrived(k):
            src = source(k)
            there = qr.at[p, :, slot_at(src, side)]
            rcopy(there, there, qsend.at[p, k], qrecv.at[p, src], tp=src).wait_recv()

        each(query_arrived)
        for hh in range(2):
            turned = mm(perm[...], qr[p, hh].reshape(256, LAT)).astype(BF)
            turned = turned.reshape(2, 8, 16, LAT)
            for s in range(STEPS):
                first = 16 * (2 * s + hh)
                qrow[:, first : first + 16, :] = turned[s]

        def attend_row(i, carry):
            r = 8 * p + i
            q_lat, q_rope, keys = qrow[i], qro[r], cache[r]
            score = mm(q_lat, keys, ((1,), (1,))) + mm(q_rope, kr[r], ((1,), (1,)))
            score = jnp.where(position < len_ref[0, r], score * SCALING, -jnp.inf)
            top = jnp.max(score, axis=1, keepdims=True)
            lat32, rope32 = q_lat.astype(F32), q_rope.astype(F32)
            news = []
            for t in range(STEPS):
                tok_r = toks[t, pl.ds(r, 1), :]
                new = jnp.sum(lat32 * tok_r[:, :LAT], axis=1, keepdims=True)
                new = new + jnp.sum(rope32 * tok_r[:, LAT:], axis=1, keepdims=True)
                new = new * SCALING
                if t == 1:
                    new = jnp.where(late, new, -jnp.inf)
                news.append((new, tok_r[:, :LAT]))
            for new, _ in news:
                top = jnp.maximum(top, new)
            expped = jnp.exp(score - top)
            new_exp = [jnp.exp(new - top) for new, _ in news]
            total = jnp.sum(expped, axis=1, keepdims=True)
            for e in new_exp:
                total = total + e
            inverse = 1.0 / total
            out = mm((expped * inverse).astype(BF), keys)
            for e, (_, tok_r) in zip(new_exp, news):
                out = out + (e * inverse).astype(BF).astype(F32) * tok_r
            out = out.astype(BF)
            for s in range(STEPS):
                for hh in range(2):
                    first = 16 * (2 * s + hh)
                    attr[hh, 8 * s + i] = out[first : first + 16]
            return carry

        lax.fori_loop(0, 8, attend_row, 0, unroll=4)
        for hh in range(2):
            turned = mm(perm[...], attr[hh].reshape(256, LAT)).astype(BF)
            ab[p, hh] = turned.reshape(2, 8, 16, LAT)
        each_kin(lambda j: back_copy(p, j).start())
        for hh in range(2):
            for f in range(2):
                ar[p, hh, f, rows16(mine), :] = ab[p, hh, f, mine]

    def heads_out(p):
        def back_arrived(j):
            m, t = kin(8 - j)
            there = ar.at[p, :, :, rows16(m), :]
            rcopy(there, there, asend.at[p, j], arecv.at[p, m], tp=t).wait_recv()

        each_kin(back_arrived)
        for f in range(2):
            for hh in range(2):
                first = 256 * f + VDIM * hh
                ho[p, :, first : first + VDIM] = mm(
                    ar[p, hh, f], vm[f, :, hh * VDIM : (hh + 1) * VDIM]
                ).astype(BF)
        for dy in (1, 2, 3):
            gather_copy(p, dy).start()
        hg[p, 0] = ho[p]

    def multiply(p):
        for dy in (1, 2, 3):
            src = rem(y + dy, YS)
            there = hg.at[p, dy]
            rcopy(there, there, hsend.at[p, dy], hrecv.at[p, dy], tp=src * ZS + z).wait_recv()
        for q in (2 * p, 2 * p + 1):
            for first, width in ((0, 512), (512, 384)):
                cols = slice(HALF * (q % 2) + first, HALF * (q % 2) + first + width)
                total = mm(hg[p, 0], wp[0, :, cols])
                for k in range(1, YS):
                    total = total + mm(hg[p, k], wp[k, :, cols])
                pb[q, :, :, :, first : first + width] = total.astype(BF).reshape(YS, 2, 16, width)
            each_kin(lambda j: home_copy(q, j).start())
            hl[q, y, par] = pb[q, y, par]

    def home_arrived(q, j):
        m, t = kin(8 - j)
        there = hl.at[q, div(m, 2), rem(m, 2)]
        rcopy(there, there, fsend.at[q, j], frecv.at[q, m], tp=t).wait_recv()

    attend(0)
    value_copy().start()
    share_weights(0)
    attend(1)
    share_weights(1)
    value_copy().wait_recv()
    heads_out(0)
    heads_out(1)
    load_w.wait()
    for f in range(2):
        weights_arrived(f)
    multiply(0)
    multiply(1)

    for q in range(CHUNKS):
        each_kin(lambda j: home_arrived(q, j))
    for side_cols in range(2):
        for yy in range(YS):
            first = COLS * yy + HALF * side_cols
            top, low = (
                hl[q, yy, 0].astype(F32) + hl[q, yy, 1].astype(F32) for q in (side_cols, 2 + side_cols)
            )
            for s in range(STEPS):
                rows = slice(8 * s, 8 * s + 8)
                both = jnp.concatenate([top[rows], low[rows]], axis=0)
                dec[s, 0, :, first : first + HALF] = both.astype(BF)

    store_served.wait()

    for copy in sent:
        copy.wait_send()
    each(lambda k: pick_copy(k).wait_send())
    swap_bucket().wait_send()
    each(lambda k: rope_copy(k).wait_send())
    for f in range(2):
        for dy in range(1 - f, YS):
            weight_copy(f, dy).wait_send()
        for dx in range(4):
            if dx > 0:
                spread_copy(f, dx).wait_send()
            core_copy(f, dx).wait_send()
    value_copy().wait_send()
    for p in range(PARTS):
        each(lambda k: query_copy(p, k).wait_send())
        each_kin(lambda j: back_copy(p, j).wait_send())
        for dy in (1, 2, 3):
            gather_copy(p, dy).wait_send()
    for q in range(CHUNKS):
        each_kin(lambda j: home_copy(q, j).wait_send())


def hand_over(*refs):
    for source, result in zip(refs[:3], refs[3:]):
        result[...] = source[...]


def local(
    trainer_weight,
    bucket_slot,
    bucket_version,
    replica_version,
    old_weight,
    old_scale,
    q_nope,
    q_rope,
    cache_latent,
    cache_rope,
    new_token,
    lengths,
    out_weight,
):
    dma = pltpu.SemaphoreType.DMA
    results = pl.pallas_call(
        everything,
        out_shape=(
            jax.ShapeDtypeStruct((1, LAT, 512), BF),
            jax.ShapeDtypeStruct((1, 4, 4), F32),
            jax.ShapeDtypeStruct((STEPS, 1, 16, D), BF),
        ),
        in_specs=[SM] * 5 + [HB] * 8,
        out_specs=(HB, VM, VM),
        scratch_shapes=[
            pltpu.VMEM((LAT, 512), BF),
            pltpu.VMEM((HEADS, 32, 256), BF),
            pltpu.VMEM((TP, 32, 256), BF),
            pltpu.VMEM((2, LAT, 256), BF),
            pltpu.VMEM((LAT, 512), BF),
            pltpu.VMEM((LAT, 256), BF),
            pltpu.VMEM((2, LAT, 256), BF),
            pltpu.VMEM((STEPS, 256, 256), BF),
            pltpu.VMEM((PARTS, 256, 256), BF),
            pltpu.VMEM((ROWS_DEV, LEN * ROPE), BF),
            pltpu.VMEM((STEPS, ROWS_DEV, LAT + ROPE), BF),
            pltpu.VMEM((ROWS_DEV, LEN, LAT), BF),
            pltpu.VMEM((YS, 512, COLS), BF),
            pltpu.VMEM((256, 256), BF),
            pltpu.VMEM((ROWS_DEV, LEN // 2, 128), BF),
            pltpu.VMEM((ROWS_DEV, LEN, 128), BF),
            pltpu.VMEM((STEPS, ROWS_DEV, 640), F32),
            pltpu.VMEM((PARTS, 2, 256, LAT), BF),
            pltpu.VMEM((PARTS, 2, TP, 16, LAT), BF),
            pltpu.VMEM((STEPS, TP, 16, 128), BF),
            pltpu.VMEM((8, 2 * HEADS, LAT), BF),
            pltpu.VMEM((ROWS_DEV, 2 * HEADS, 128), BF),
            pltpu.VMEM((2, 16, 16, LAT), BF),
            pltpu.VMEM((PARTS, 2, 2, 8, 16, LAT), BF),
            pltpu.VMEM((PARTS, 2, 2, 128, LAT), BF),
            pltpu.VMEM((PARTS, 128, 512), BF),
            pltpu.VMEM((PARTS, YS, 128, 512), BF),
            pltpu.VMEM((CHUNKS, YS, 2, 16, HALF), BF),
            pltpu.VMEM((CHUNKS, YS, 2, 16, HALF), BF),
            dma((9,)),
            dma((15,)),
            dma((REPS,)),
            dma((TP,)),
            dma((TP,)),
            dma(()),
            dma(()),
            dma((2, YS)),
            dma((2, YS)),
            dma((2, 4)),
            dma((2, 4)),
            dma((2, 4)),
            dma((2, 4)),
            dma(()),
            dma(()),
            dma((TP,)),
            dma((TP,)),
            dma((PARTS, TP)),
            dma((PARTS, TP)),
            dma((PARTS, 8)),
            dma((PARTS, 8)),
            dma((PARTS, YS)),
            dma((PARTS, YS)),
            dma((CHUNKS, 8)),
            dma((CHUNKS, 8)),
        ],
        compiler_params=pltpu.CompilerParams(
            collective_id=0, has_side_effects=True, vmem_limit_bytes=56 * 2**20
        ),
        name="push_and_decode",
    )(
        bucket_slot,
        bucket_version,
        replica_version,
        old_scale,
        lengths,
        trainer_weight,
        old_weight,
        q_nope,
        q_rope,
        cache_latent,
        cache_rope,
        new_token,
        out_weight,
    )
    return pl.pallas_call(
        hand_over,
        out_shape=tuple(jax.ShapeDtypeStruct(r.shape, r.dtype) for r in results),
        in_specs=[VM] * 3,
        out_specs=(VM,) * 3,
        compiler_params=pltpu.CompilerParams(vmem_limit_bytes=56 * 2**20),
        name="hand_over",
    )(*results)


def solution(mesh):
    return jax.shard_map(
        local,
        mesh=mesh,
        in_specs=(
            P("rep", "tp", None),
            P(),
            P(),
            P("rep", None),
            P("rep", None, "tp"),
            P("rep", None, "tp"),
            P(None, "rep", None, "tp"),
            P(None, "rep", None, "tp"),
            P("rep", "tp", None, None),
            P("rep", "tp", None),
            P(None, "rep", "tp", None),
            P("rep", "tp"),
            P("tp", None),
        ),
        out_specs=(P("rep", None, "tp"), P("rep", None, "tp"), P(None, "rep", "tp", None)),
        check_vma=False,
    )
```
